256 devices in a mesh: expert: 64 (over x, z, core), tensor: 4 (over y).
Axes of the slice: x: 4, y: 4, z: 8, core: 2. Of those that a mesh axis runs over, the one named last changes fastest.
Arguments:
- query_latent: bfloat16 [2048, 128, 512], P('expert', 'tensor'), may hold values from -82 to 82
- query_rope: bfloat16 [2048, 8192], P('expert', 'tensor'), may hold values from -5 to 5
- cache_latent: bfloat16 [2048, 128, 512], P('expert'), may hold values from -5 to 5
- cache_rope: bfloat16 [2048, 64, 128], P('expert'), may hold values from -5 to 5
- cache_len: int32 [2048], P('expert'), may hold values from 2 to 128
- moe_input: bfloat16 [2048, 3584], P(('expert', 'tensor')), may hold values from -6 to 6
- routes: int32 [2048, 8], P(('expert', 'tensor')), may hold values from 0 to 63, all different within a row; in each aligned block of 8 rows (0 to 7, 8 to 15, ...) at most 2 rows name the same one
- gate_weights: float32 [2048, 8], P(('expert', 'tensor')), may hold values from 0.1 to 0.5
- w_gate: bfloat16 [64, 3584, 1024], P('expert', None, 'tensor'), may hold values from -0.09375 to 0.09375
- w_up: bfloat16 [64, 3584, 1024], P('expert', None, 'tensor'), may hold values from -0.09375 to 0.09375
- w_down: bfloat16 [64, 1024, 3584], P('expert', 'tensor'), may hold values from -0.1875 to 0.1875
Outputs:
- context: bfloat16 [2048, 128, 512], P(('expert', 'tensor'))
- moe_output: bfloat16 [2048, 3584], P(('expert', 'tensor'))
The draws below stay inside these ranges and needn't reach their ends.
Inputs may be any that keep to these rules, and one draw needn't show every extreme that they name: `routes`: each row names 8 different experts; in each aligned block of 8 rows (the rows of one device) no expert is named by more than 2 rows.
All inputs are finite; a program needn't handle non-finite values.
Results may differ from the reference program's by a relative error of at most 0.012.
Values may be sent and summed in bfloat16 or wider, within the bound.
No kernel may reach another device: no remote copies, remote signals or barrier semaphores. Data moves between devices by JAX's collectives and lax.ppermute only.
A program may use at most 128 MiB of HBM per device.

```python
import math
import jax
import jax.numpy as jnp
import numpy as np
from jax import lax

D = 3584
HEADS = 128
LATENT = 512
ROPE = 64
FFW = 1024
TOPK = 8
ROW_DEV = 8
CTX = 128
EXPERTS = 64
CAP = 2
ROWS_GRP = 32
ROWS = 2048


def leading_keys(key):
    return jnp.clip(jax.random.normal(jax.random.fold_in(key, 5), (ROWS, 2, LATENT), jnp.float32), -5.0, 5.0)


def draw_cache_latent(key, part):
    leading = leading_keys(key)
    key = jax.random.fold_in(key, 31)
    others = jnp.clip(jax.random.normal(key, (ROWS, CTX, LATENT), jnp.float32), -5.0, 5.0)
    return jnp.concatenate([leading, others[:, 2:]], axis=1).astype(jnp.bfloat16)


def draw_query_latent(key, part):
    key = jax.random.fold_in(key, 37)
    query = jnp.clip(jax.random.normal(key, (ROWS, HEADS, LATENT), jnp.float32), -5.0, 5.0)
    return query.astype(jnp.bfloat16)


def draw_query_rope(key, part):
    key = jax.random.fold_in(key, 43)
    query = jnp.clip(jax.random.normal(key, (ROWS, HEADS, ROPE), jnp.float32), -5.0, 5.0)
    return query.reshape(ROWS, HEADS * ROPE).astype(jnp.bfloat16)


def draw_cache_len(key, part):
    key = jax.random.fold_in(key, 47)
    lengths = jax.random.randint(key, (ROWS,), 2, CTX + 1, jnp.int32)
    spot = jax.random.randint(jax.random.fold_in(key, 1), (), 0, ROWS, jnp.int32)
    return lengths.at[spot].set(CTX)


def block_scale(key, dims, split, low, top_value):
    def one(axis_at, parts):
        steps = jax.random.uniform(jax.random.fold_in(jax.random.fold_in(key, 6), axis_at), (parts,), jnp.float32, low / len(split), top_value / len(split))
        return jnp.repeat(jnp.exp(steps), dims[axis_at] // parts).reshape((-1,) + (1,) * (len(dims) - axis_at - 1))

    loudness = one(*split[0])
    for cut in split[1:]:
        loudness = loudness * one(*cut)
    return loudness


def deal_out(key, own, number, rows, amount, top, bound, skew):
    ranking = jax.random.permutation(key, amount)
    crowded, usual = load_shares(amount, rows * top, bound, skew, True), load_shares(amount, rows * top, bound, skew, False)
    places = jnp.arange(amount)

    def named(sizes, offset_by):
        used = int((sizes > 0).sum())
        fixed = max(1, used // 4)
        shifted = fixed + (places - fixed + offset_by * (used - fixed)) % max(1, amount - fixed)
        return jnp.zeros((amount,), jnp.int32).at[ranking[jnp.where(places < fixed, places, shifted)]].set(jnp.asarray(sizes, jnp.int32))

    sizes = jnp.where(number % 4 == 0, named(crowded, number // 4), named(usual, number - number // 4 - 1))
    mixed = jax.random.permutation(jax.random.fold_in(own, 3), amount)
    donor, receiver = mixed[0:amount // 2 * 2:2], mixed[1:amount // 2 * 2:2]
    margin = jnp.minimum(sizes[donor] - 1, bound - sizes[receiver]) // 2
    margin = jnp.where((donor == ranking[0]) | (receiver == ranking[0]) | (sizes[receiver] == 0), 0, jnp.maximum(margin, 0))
    shifted = jax.random.randint(jax.random.fold_in(own, 4), (amount // 2,), 0, 1 << 20) % (margin + 1)
    sizes = sizes.at[donor].add(-shifted).at[receiver].add(shifted)
    labels = jnp.searchsorted(jnp.cumsum(sizes), jnp.arange(rows * top), side="right").astype(jnp.int32)
    listing = labels.reshape(top, rows).T
    listing = listing[jax.random.permutation(jax.random.fold_in(own, 1), rows)]
    offset_by = jax.random.randint(jax.random.fold_in(own, 2), (rows, 1), 0, top)
    return jnp.take_along_axis(listing, (jnp.arange(top)[None, :] + offset_by) % top, axis=1)


def load_shares(number_of, total, limit, skew, full):
    weights = [(1 << 20) // math.isqrt(grade ** skew) + 1 for grade in range(1, number_of + 1)]
    largest = limit if full else min(limit, max(-(-total // number_of), total * weights[0] // sum(weights)))
    least = 1 if total - largest >= number_of - 1 else 0
    given, spare = [largest] + [least] * (number_of - 1), total - largest - least * (number_of - 1)
    while spare > 0:
        candidates = [i for i in range(1, number_of) if given[i] < largest] or [i for i in range(1, number_of) if given[i] < limit]
        mass, remaining = sum([weights[i] for i in candidates]), spare
        for i in candidates:
            more = min(limit - given[i], max(1, remaining * weights[i] // mass), spare)
            given[i] = given[i] + more
            spare = spare - more
    return np.array(given)


def normal_values(key, shape, width, limit, shards=(), kind=jnp.bfloat16):
    entries = jax.random.normal(key, shape, jnp.float32) * width
    if len(shards) > 0:
        entries = block_scale(key, shape, shards, -0.22, 0.18) * entries
    return jnp.clip(entries, min=-limit, max=limit).astype(kind)


def setup_inputs(seed: int = 0) -> dict:
    streams_of = jax.random.split(jax.random.key(seed), 12)
    query_latent = draw_query_latent(jax.random.fold_in(streams_of[11], 71), 0)
    query_rope = draw_query_rope(jax.random.fold_in(streams_of[11], 71), 0)
    cache_latent = draw_cache_latent(jax.random.fold_in(streams_of[11], 71), 0)
    cache_rope = normal_values(streams_of[3], (ROWS, ROPE, CTX), 1.0, 5.0, ((0, 64),))
    cache_len = draw_cache_len(jax.random.fold_in(streams_of[11], 71), 0)
    moe_input = normal_values(streams_of[5], (ROWS, D), 1.0, 6.0, ((0, 256),))
    routes_keys = jax.random.split(jax.random.fold_in(streams_of[6], 1), ROWS // ROW_DEV)
    routes_turns = jax.random.permutation(jax.random.fold_in(streams_of[6], 3), ROWS // ROW_DEV)
    routes = jax.vmap(lambda own, number: deal_out(jax.random.fold_in(streams_of[6], 2), own, number, ROW_DEV, EXPERTS, TOPK, CAP, 2))(routes_keys, routes_turns).reshape((ROWS, TOPK))
    gate_weights = jnp.clip(0.1 + 0.4 * jax.random.uniform(streams_of[7], (ROWS, TOPK), jnp.float32) ** block_scale(streams_of[7], (ROWS, TOPK), ((0, 256),), -0.2, 0.2), 0.1, 0.5)
    w_gate = normal_values(streams_of[8], (EXPERTS, D, FFW), D ** -0.5, 0.09375, ((0, 64), (2, 4)))
    w_up = normal_values(streams_of[9], (EXPERTS, D, FFW), D ** -0.5, 0.09375, ((0, 64), (2, 4)))
    w_down = normal_values(streams_of[10], (EXPERTS, FFW, D), FFW ** -0.5, 0.1875, ((0, 64), (1, 4)))
    return {"query_latent": query_latent, "query_rope": query_rope, "cache_latent": cache_latent, "cache_rope": cache_rope, "cache_len": cache_len, "moe_input": moe_input, "routes": routes, "gate_weights": gate_weights, "w_gate": w_gate, "w_up": w_up, "w_down": w_down}


score_scale = 192.0 ** -0.5
block_rows = 128


def attend(query_latent, query_rope, cache_latent, cache_rope, cache_len):
    count = query_latent.shape[0]
    scores = jnp.einsum("rhl,rpl->rhp", query_latent.astype(jnp.float32), cache_latent.astype(jnp.float32))
    rotary = query_rope.reshape(count, HEADS, ROPE).astype(jnp.float32)
    scores = scores + jnp.einsum("rhe,rep->rhp", rotary, cache_rope.astype(jnp.float32))
    scores = scores * score_scale
    valid = jnp.arange(CTX, dtype=jnp.int32)[None, None, :] < cache_len[:, None, None]
    scores = jnp.where(valid, scores, -1e30)
    highest = jnp.max(scores, axis=-1, keepdims=True)
    powers = jnp.exp(scores - highest)
    weights = (powers / jnp.sum(powers, axis=-1, keepdims=True)).astype(jnp.bfloat16)
    mixed = jnp.einsum("rhp,rpl->rhl", weights.astype(jnp.float32), cache_latent.astype(jnp.float32))
    return mixed.astype(jnp.bfloat16)


def reference(query_latent, query_rope, cache_latent, cache_rope, cache_len, moe_input, routes, gate_weights, w_gate, w_up, w_down):
    groups = ROWS // ROWS_GRP
    stacked = (query_latent.reshape(groups, ROWS_GRP, HEADS, LATENT),
               query_rope.reshape(groups, ROWS_GRP, HEADS * ROPE),
               cache_latent.reshape(groups, ROWS_GRP, CTX, LATENT),
               cache_rope.reshape(groups, ROWS_GRP, ROPE, CTX),
               cache_len.reshape(groups, ROWS_GRP))

    def one_group(pieces):
        return attend(pieces[0], pieces[1], pieces[2], pieces[3], pieces[4])

    context = lax.map(one_group, stacked).reshape(ROWS, HEADS, LATENT)

    assigned = ROWS * TOPK
    flat = routes.reshape(-1).astype(jnp.int32)
    load = (ROWS // ROW_DEV) * CAP
    padded = ((load + block_rows - 1) // block_rows) * block_rows

    def per_expert(expert, outputs):
        chosen = flat == expert
        where_ids = jnp.nonzero(chosen, size=padded, fill_value=assigned)[0].astype(jnp.int32)
        number = jnp.sum(chosen.astype(jnp.int32))
        gate_mat = w_gate[expert]
        up_mat = w_up[expert]
        down_mat = w_down[expert]

        def per_block(index, outputs):
            start = (index * block_rows).astype(jnp.int32)
            ids = lax.dynamic_slice_in_dim(where_ids, start, block_rows)
            picked = moe_input[jnp.minimum(ids, assigned - 1) // TOPK]
            gate = jnp.dot(picked, gate_mat, preferred_element_type=jnp.float32)
            upper = jnp.dot(picked, up_mat, preferred_element_type=jnp.float32)
            hidden = (jax.nn.silu(gate) * upper).astype(jnp.bfloat16)
            result = jnp.dot(hidden, down_mat, preferred_element_type=jnp.float32).astype(jnp.bfloat16)
            return outputs.at[ids].set(result, mode="drop")

        blocks = ((number + block_rows - 1) // block_rows).astype(jnp.int32)
        return lax.fori_loop(jnp.int32(0), blocks, per_block, outputs)

    outputs = lax.fori_loop(0, EXPERTS, per_expert, jnp.zeros((assigned, D), jnp.bfloat16))
    expert_out = outputs.reshape(ROWS, TOPK, D).astype(jnp.float32)
    moe_output = jnp.sum(gate_weights[:, :, None] * expert_out, axis=1).astype(jnp.bfloat16)
    return context, moe_output
```

```python
import jax
import jax.numpy as jnp
from jax import lax
from jax.sharding import PartitionSpec as P

score_scale = 192.0 ** (-0.5)
CAP = 2


def attend(query_latent, query_rope, cache_latent, cache_rope, cache_len):
    count, heads, latent = query_latent.shape
    rotary_width = cache_rope.shape[1]
    positions = cache_latent.shape[1]
    rotary = query_rope.reshape(count, heads, rotary_width)
    scores = jnp.einsum(
        "rhl,rpl->rhp", query_latent, cache_latent, preferred_element_type=jnp.float32
    )
    scores = scores + jnp.einsum(
        "rhe,rep->rhp", rotary, cache_rope, preferred_element_type=jnp.float32
    )
    scores = scores * score_scale
    valid = jnp.arange(positions, dtype=jnp.int32)[None, None, :] < cache_len[:, None, None]
    scores = jnp.where(valid, scores, -1e30)
    highest = jnp.max(scores, axis=-1, keepdims=True)
    powers = jnp.exp(scores - highest)
    weights = (powers / jnp.sum(powers, axis=-1, keepdims=True)).astype(jnp.bfloat16)
    mixed = jnp.einsum("rhp,rpl->rhl", weights, cache_latent, preferred_element_type=jnp.float32)
    return mixed.astype(jnp.bfloat16)


def split3(v):
    high = v.astype(jnp.bfloat16)
    rest = v - high.astype(jnp.float32)
    middle = rest.astype(jnp.bfloat16)
    low = (rest - middle.astype(jnp.float32)).astype(jnp.bfloat16)
    return high, middle, low


def slot_masks(routes, experts):
    named = jnp.any(routes[..., None] == jnp.arange(experts, dtype=jnp.int32), axis=-2)
    rows = routes.shape[-2]
    counts = named.astype(jnp.int32)
    earlier = [jnp.zeros_like(counts[..., 0, :])]
    for row in range(1, rows):
        earlier.append(earlier[-1] + counts[..., row - 1, :])
    earlier = jnp.stack(earlier, axis=-2)
    return named[..., None] & (earlier[..., None] == jnp.arange(CAP, dtype=jnp.int32))


def per_device(
    query_latent,
    query_rope,
    cache_latent,
    cache_rope,
    cache_len,
    moe_input,
    routes,
    gate_weights,
    w_gate,
    w_up,
    w_down,
):
    bf16, f32 = jnp.bfloat16, jnp.float32
    shares = lax.axis_size("tensor")
    experts = lax.axis_size("expert")
    me = lax.axis_index("tensor")
    rows, width = moe_input.shape
    chosen = routes.shape[1]
    units = w_gate.shape[2]
    part = width // shares
    slots = experts * CAP

    def shift(value, by):
        pairs = [(i, (i + by) % shares) for i in range(shares)]
        return lax.ppermute(value, "tensor", pairs)

    own_mask = slot_masks(routes, experts)
    select = jnp.transpose(own_mask, (1, 2, 0)).reshape(slots, rows).astype(bf16)
    packed = jnp.dot(select, moe_input, preferred_element_type=f32).astype(bf16)
    down_parts = [
        lax.dynamic_slice(w_down[0], (0, ((me + by) % shares) * part), (units, part))
        for by in range(shares)
    ]
    down = [down_parts[0]] + [shift(down_parts[by], by) for by in range(1, shares)]
    small = jnp.concatenate([routes.astype(f32), gate_weights], axis=1)
    group = jnp.stack([small] + [shift(small, by) for by in range(1, shares)])

    received = lax.all_to_all(
        packed.reshape(experts, CAP, width), "expert", split_axis=0, concat_axis=0, tiled=True
    ).reshape(slots, width)

    half = slots // 2
    block1 = shift(received, 1)
    block3 = shift(received, 3)
    block2 = jnp.concatenate([shift(block1[:half], 1), shift(block3[half:], 3)], axis=0)

    def hidden_of(block):
        gate = jnp.dot(block, w_gate[0], preferred_element_type=f32)
        upper = jnp.dot(block, w_up[0], preferred_element_type=f32)
        return (jax.nn.silu(gate) * upper).astype(bf16)

    hidden = [hidden_of(b) for b in (received, block1, block2, block3)]
    own_hidden = jnp.stack(hidden)
    gathered = [own_hidden] + [shift(own_hidden, by) for by in range(1, shares)]
    all_hidden = jnp.stack(
        [
            jnp.concatenate([gathered[s][(d - s) % shares] for s in range(shares)], axis=1)
            for d in range(shares)
        ],
        axis=0,
    )
    all_hidden = all_hidden.reshape(shares, experts, CAP, shares * units)
    all_hidden = jnp.transpose(all_hidden, (1, 0, 2, 3)).reshape(slots * shares, shares * units)
    expert_out = jnp.dot(
        all_hidden, jnp.concatenate(down, axis=0), preferred_element_type=f32
    ).astype(bf16)

    local_context = attend(query_latent, query_rope, cache_latent, cache_rope, cache_len)
    heads, latent = local_context.shape[1:]
    context_parts = [
        lax.dynamic_slice(
            local_context, (((me + by) % shares) * rows, 0, 0), (rows, heads, latent)
        )
        for by in range(shares)
    ]
    context_parts = [context_parts[0]] + [
        shift(context_parts[by], by) for by in range(1, shares)
    ]

    returned = lax.all_to_all(
        expert_out.reshape(experts, shares * CAP, part),
        "expert",
        split_axis=0,
        concat_axis=0,
        tiled=True,
    ).reshape(experts * shares * CAP, part)

    group_mask = slot_masks(group[:, :, :chosen].astype(jnp.int32), experts)
    group_routes = group[:, :, :chosen].astype(jnp.int32)
    match = group_routes[..., None] == jnp.arange(experts, dtype=jnp.int32)
    gates = jnp.sum(jnp.where(match, group[:, :, chosen:, None], 0.0), axis=2)
    weight = jnp.where(group_mask, gates[..., None], 0.0)
    same = jnp.arange(shares)[:, None] == jnp.arange(shares)[None, :]
    combine = jnp.where(same[:, None, None, :, None], weight[:, :, :, None, :], 0.0)
    combine = combine.reshape(shares * rows, experts * shares * CAP)
    sums = jnp.dot(
        jnp.concatenate(split3(combine), axis=0), returned, preferred_element_type=f32
    ).reshape(3, shares, rows, part)
    sums = (sums[2] + sums[1] + sums[0]).astype(bf16)
    pieces = [sums[0]] + [shift(sums[d], shares - d) for d in range(1, shares)]
    wide = jnp.concatenate(pieces + pieces, axis=1)
    moe_output = lax.dynamic_slice(wide, (0, ((shares - me) % shares) * part), (rows, width))

    context = jnp.zeros((rows, shares, heads, latent), bf16)
    for by in range(shares):
        context = lax.dynamic_update_slice(
            context, context_parts[by][:, None], (0, (me - by) % shares, 0, 0)
        )
    return (context.reshape(rows, shares * heads, latent), moe_output)


def solution(mesh):
    return jax.shard_map(
        per_device,
        mesh=mesh,
        in_specs=(
            P("expert", "tensor", None),
            P("expert", "tensor"),
            P("expert", None, None),
            P("expert", None, None),
            P("expert"),
            P(("expert", "tensor"), None),
            P(("expert", "tensor"), None),
            P(("expert", "tensor"), None),
            P("expert", None, "tensor"),
            P("expert", None, "tensor"),
            P("expert", "tensor", None),
        ),
        out_specs=(P(("expert", "tensor"), None, None), P(("expert", "tensor"), None)),
        check_vma=False,
    )
```

```python
import functools

import jax
import jax.numpy as jnp
from jax import lax
from jax.experimental import pallas as pl
from jax.experimental.pallas import tpu as pltpu
from jax.sharding import PartitionSpec as P

score_scale = 192.0 ** (-0.5)
CAP = 2
INFO = 16


def attend(query_latent, query_rope, cache_latent, cache_rope, cache_len):
    count, heads, latent = query_latent.shape
    rotary_width = cache_rope.shape[1]
    positions = cache_latent.shape[1]
    rotary = query_rope.reshape(count, heads, rotary_width)
    scores = jnp.einsum(
        "rhl,rpl->rhp", query_latent, cache_latent, preferred_element_type=jnp.float32
    )
    scores = scores + jnp.einsum(
        "rhe,rep->rhp", rotary, cache_rope, preferred_element_type=jnp.float32
    )
    scores = scores * score_scale
    valid = jnp.arange(positions, dtype=jnp.int32)[None, None, :] < cache_len[:, None, None]
    scores = jnp.where(valid, scores, -1e30)
    highest = jnp.max(scores, axis=-1, keepdims=True)
    powers = jnp.exp(scores - highest)
    weights = (powers / jnp.sum(powers, axis=-1, keepdims=True)).astype(jnp.bfloat16)
    mixed = jnp.einsum("rhp,rpl->rhl", weights, cache_latent, preferred_element_type=jnp.float32)
    return mixed.astype(jnp.bfloat16)


def split3(v):
    high = v.astype(jnp.bfloat16)
    rest = v - high.astype(jnp.float32)
    middle = rest.astype(jnp.bfloat16)
    low = (rest - middle.astype(jnp.float32)).astype(jnp.bfloat16)
    return high, middle, low


def slot_masks(routes, experts):
    named = jnp.any(routes[..., None] == jnp.arange(experts, dtype=jnp.int32), axis=-2)
    rows = routes.shape[-2]
    counts = named.astype(jnp.int32)
    earlier = [jnp.zeros_like(counts[..., 0, :])]
    for row in range(1, rows):
        earlier.append(earlier[-1] + counts[..., row - 1, :])
    earlier = jnp.stack(earlier, axis=-2)
    return named[..., None] & (earlier[..., None] == jnp.arange(CAP, dtype=jnp.int32))


vmem_params = pltpu.CompilerParams(vmem_limit_bytes=40 * 1024 * 1024)
whole = pl.BlockSpec(memory_space=pltpu.VMEM)


def pack_kernel(shares, experts, routes_ref, rows_ref, out_ref):
    f32, bf16 = jnp.float32, jnp.bfloat16
    rows, width = rows_ref.shape
    part = width // shares
    chunk = shares * CAP
    lane = lax.broadcasted_iota(jnp.int32, (rows, experts * chunk), 1)
    expert, slot, quarter = lane // chunk, lane % CAP, lane % chunk // CAP
    named = jnp.zeros(lane.shape, f32)
    for k in range(routes_ref.shape[1]):
        named = jnp.where(routes_ref[:, k : k + 1] == expert, 1.0, named)
    before = lax.broadcasted_iota(jnp.int32, (rows, rows), 0) > lax.broadcasted_iota(
        jnp.int32, (rows, rows), 1
    )
    earlier = jnp.dot(before.astype(f32), named, preferred_element_type=f32)
    taken = jnp.where(earlier == slot.astype(f32), named, 0.0)
    select = jnp.concatenate(
        [jnp.where(quarter == q, taken, 0.0) for q in range(shares)], axis=0
    )
    values = rows_ref[...].astype(f32)
    values = jnp.concatenate(
        [values[:, q * part : (q + 1) * part] for q in range(shares)], axis=0
    )
    out_ref[...] = jnp.dot(
        select.T.astype(bf16), values.astype(bf16), preferred_element_type=f32
    ).astype(bf16)


def pack_rows(routes, rows, shares, experts):
    part = rows.shape[1] // shares
    total = experts * shares * CAP
    return pl.pallas_call(
        functools.partial(pack_kernel, shares, experts),
        out_shape=jax.ShapeDtypeStruct((total, part), rows.dtype),
        in_specs=[whole] * 2,
        out_specs=whole,
        compiler_params=vmem_params,
        cost_estimate=pl.CostEstimate(
            flops=2 * total * part * rows.shape[0] * shares,
            bytes_accessed=2 * total * part,
            transcendentals=0,
        ),
    )(routes, rows)


def hidden_kernel(count, shares, *refs):
    halves, (order_ref, gate_ref, up_ref, out_ref, wide) = refs[:count], refs[count:]
    rows, part = halves[0].shape
    slots = rows // shares
    for h in range(count):
        ordered = jnp.dot(
            order_ref[...], halves[h][...], preferred_element_type=jnp.float32
        ).astype(wide.dtype)
        for q in range(shares):
            wide[pl.ds(h * slots, slots), pl.ds(q * part, part)] = ordered[
                q * slots : (q + 1) * slots
            ]
    gate = jnp.dot(wide[...], gate_ref[...], preferred_element_type=jnp.float32)
    upper = jnp.dot(wide[...], up_ref[...], preferred_element_type=jnp.float32)
    out_ref[...] = (gate / (1.0 + jnp.exp(-gate)) * upper).astype(out_ref.dtype)


def hidden_units(halves, order, w_gate, w_up):
    count = len(halves)
    rows, part = halves[0].shape
    width, units = w_gate.shape
    shares = width // part
    total = count * rows // shares
    return pl.pallas_call(
        functools.partial(hidden_kernel, count, shares),
        out_shape=jax.ShapeDtypeStruct((total, units), jnp.bfloat16),
        in_specs=[whole] * (count + 3),
        out_specs=whole,
        scratch_shapes=[pltpu.VMEM((total, width), jnp.bfloat16)],
        compiler_params=vmem_params,
        cost_estimate=pl.CostEstimate(
            flops=4 * total * width * units,
            bytes_accessed=4 * width * units + 2 * total * width,
            transcendentals=total * units,
        ),
    )(*halves, order, w_gate, w_up)


def down_early_kernel(shares, *refs):
    early, weights, out_ref = refs[:shares], refs[shares : 2 * shares], refs[2 * shares]
    slots = out_ref.shape[0] // shares
    for block in range(shares):
        total = None
        for s in range(shares):
            of_sender = (block - s) % shares
            if of_sender == shares // 2:
                continue
            place = of_sender - (of_sender > shares // 2)
            units = early[s][pl.ds(place * slots, slots), :]
            term = jnp.dot(
                units, weights[s][: units.shape[1], :], preferred_element_type=jnp.float32
            )
            total = term if total is None else total + term
        out_ref[pl.ds(block * slots, slots), :] = total


def down_late_kernel(shares, *refs):
    late, weights = refs[:shares], refs[shares : 2 * shares]
    early_ref, order_ref, out_ref, plain = refs[2 * shares :]
    slots = late[0].shape[0]
    half = slots // 2
    for block in range(shares):
        s = (block - shares // 2) % shares
        units = late[s][...]
        term = jnp.dot(
            units, weights[s][: units.shape[1], :], preferred_element_type=jnp.float32
        )
        total = (early_ref[pl.ds(block * slots, slots), :] + term).astype(plain.dtype)
        plain[pl.ds(block * half, half), :] = total[:half]
        plain[pl.ds((shares + block) * half, half), :] = total[half:]
    for h in range(2):
        place = pl.ds(h * shares * half, shares * half)
        out_ref[place, :] = jnp.dot(
            order_ref[...], plain[place, :], preferred_element_type=jnp.float32
        ).astype(out_ref.dtype)


def down_early(early, weights):
    shares = len(weights)
    units, part = weights[0].shape
    rows = early[0].shape[0] // (shares - 1) * shares
    return pl.pallas_call(
        functools.partial(down_early_kernel, shares),
        out_shape=jax.ShapeDtypeStruct((rows, part), jnp.float32),
        in_specs=[whole] * (2 * shares),
        out_specs=whole,
        compiler_params=vmem_params,
        cost_estimate=pl.CostEstimate(
            flops=2 * rows * part * (shares - 1) * units,
            bytes_accessed=4 * rows * part + 4 * units * part * shares,
            transcendentals=0,
        ),
    )(*early, *weights)


def down_late(late, weights, early, order):
    shares = len(weights)
    rows, part = early.shape
    return pl.pallas_call(
        functools.partial(down_late_kernel, shares),
        out_shape=jax.ShapeDtypeStruct((rows, part), jnp.bfloat16),
        in_specs=[whole] * (2 * shares + 2),
        out_specs=whole,
        scratch_shapes=[pltpu.VMEM((rows, part), jnp.bfloat16)],
        compiler_params=vmem_params,
        cost_estimate=pl.CostEstimate(
            flops=2 * rows * part * (weights[0].shape[0] + rows),
            bytes_accessed=6 * rows * part,
            transcendentals=0,
        ),
    )(*late, *weights, early, order)


def per_device(
    query_latent,
    query_rope,
    cache_latent,
    cache_rope,
    cache_len,
    moe_input,
    routes,
    gate_weights,
    w_gate,
    w_up,
    w_down,
):
    bf16, f32 = jnp.bfloat16, jnp.float32
    shares = lax.axis_size("tensor")
    experts = lax.axis_size("expert")
    me = lax.axis_index("tensor")
    rows, width = moe_input.shape
    chosen = routes.shape[1]
    units = w_gate.shape[2]
    part = width // shares
    slots = experts * CAP

    def shift(value, by):
        pairs = [(i, (i + by) % shares) for i in range(shares)]
        return lax.ppermute(value, "tensor", pairs)

    packed = pack_rows(routes, moe_input, shares, experts)
    packed, w_down, routes, gate_weights = lax.optimization_barrier(
        (packed, w_down, routes, gate_weights)
    )
    received = lax.all_to_all(
        packed.reshape(experts, shares * CAP, part),
        "expert",
        split_axis=0,
        concat_axis=0,
        tiled=True,
    ).reshape(shares * slots, part)
    info = jnp.concatenate((routes.astype(bf16),) + split3(gate_weights), axis=1)
    info = jnp.pad(info, ((0, INFO - rows), (0, part - info.shape[1])))
    down_parts = [
        jnp.concatenate(
            [
                lax.dynamic_slice(w_down[0], (0, ((me + by) % shares) * part), (units, part)),
                info,
            ],
            axis=0,
        )
        for by in range(shares)
    ]
    down = [down_parts[0]] + [shift(down_parts[by], by) for by in range(1, shares)]
    local_context = attend(query_latent, query_rope, cache_latent, cache_rope, cache_len)
    heads, latent = local_context.shape[1:]
    received, local_context = lax.optimization_barrier((received, local_context))

    half = shares * slots // 2
    low, high = received[:half], received[half:]
    place = jnp.arange(half, dtype=jnp.int32)
    by_quarter = place // (half // shares), place % (half // shares)
    source = by_quarter[1] // CAP * (shares * CAP) + by_quarter[0] * CAP + by_quarter[1] % CAP
    sort = (source[:, None] == place[None, :]).astype(bf16)

    def hidden_of(*halves):
        return hidden_units(halves, sort, w_gate[0], w_up[0])

    low1, high3 = shift(low, 1), shift(high, 3)
    hidden0 = hidden_of(low, high)
    low, high, hidden0, down = lax.optimization_barrier((low, high, hidden0, down))
    high1, low3 = shift(high, 1), shift(low, 3)
    low2, high2 = shift(low1, 1), shift(high3, 3)
    hidden13 = hidden_of(low1, high1, low3, high3)
    early = jnp.concatenate([hidden0, hidden13], axis=0)
    early = [early] + [shift(early, by) for by in range(1, shares)]
    late = hidden_of(low2, high2)
    late = [late] + [shift(late, by) for by in range(1, shares)]

    expert_out = down_late(late, down, down_early(early, down), sort.T)
    expert_out, local_context, down = lax.optimization_barrier(
        (expert_out, local_context, down)
    )

    returned = lax.all_to_all(
        expert_out.reshape(experts, shares * CAP, part),
        "expert",
        split_axis=0,
        concat_axis=0,
        tiled=True,
    ).reshape(experts * shares * CAP, part)
    context_parts = [
        lax.dynamic_slice(
            local_context, (((me + by) % shares) * rows, 0, 0), (rows, heads, latent)
        )
        for by in range(shares)
    ]
    context_parts = [context_parts[0]] + [
        shift(context_parts[by], by) for by in range(1, shares)
    ]

    context = jnp.zeros((rows, shares, heads, latent), bf16)
    for by in range(shares):
        context = lax.dynamic_update_slice(
            context, context_parts[by][:, None], (0, (me - by) % shares, 0, 0)
        )

    info = jnp.stack([d[units : units + rows, : 4 * chosen] for d in down]).astype(f32)
    group_routes = info[:, :, :chosen].astype(jnp.int32)
    group_gates = (info[:, :, chosen : 2 * chosen] + info[:, :, 2 * chosen : 3 * chosen]) + info[
        :, :, 3 * chosen :
    ]
    group_mask = slot_masks(group_routes, experts)
    match = group_routes[..., None] == jnp.arange(experts, dtype=jnp.int32)
    gates = jnp.sum(jnp.where(match, group_gates[..., None], 0.0), axis=2)
    weight = jnp.where(group_mask, gates[..., None], 0.0)
    same = jnp.arange(shares)[:, None] == jnp.arange(shares)[None, :]
    combine = jnp.where(same[:, None, None, :, None], weight[:, :, :, None, :], 0.0)
    combine = combine.reshape(shares * rows, experts * shares * CAP)
    returned, context, combine = lax.optimization_barrier((returned, context, combine))
    sums = jnp.dot(
        jnp.concatenate(split3(combine), axis=0), returned, preferred_element_type=f32
    ).reshape(3, shares, rows, part)
    sums = (sums[2] + sums[1] + sums[0]).astype(bf16)
    pieces = [sums[0]] + [shift(sums[d], shares - d) for d in range(1, shares)]
    wide = jnp.concatenate(pieces + pieces, axis=1)
    moe_output = lax.dynamic_slice(wide, (0, ((shares - me) % shares) * part), (rows, width))

    return (context.reshape(rows, shares * heads, latent), moe_output)


def solution(mesh):
    return jax.shard_map(
        per_device,
        mesh=mesh,
        in_specs=(
            P("expert", "tensor", None),
            P("expert", "tensor"),
            P("expert", None, None),
            P("expert", None, None),
            P("expert"),
            P(("expert", "tensor"), None),
            P(("expert", "tensor"), None),
            P(("expert", "tensor"), None),
            P("expert", None, "tensor"),
            P("expert", None, "tensor"),
            P("expert", "tensor", None),
        ),
        out_specs=(P(("expert", "tensor"), None, None), P(("expert", "tensor"), None)),
        check_vma=False,
    )
```

```python
import functools

import jax
import jax.numpy as jnp
from jax import lax
from jax.experimental import pallas as pl
from jax.experimental.pallas import tpu as pltpu
from jax.sharding import PartitionSpec as P

score_scale = 192.0 ** (-0.5)
CAP = 2
INFO = 16


def attend(query_latent, query_rope, cache_latent, cache_rope, cache_len):
    count, heads, latent = query_latent.shape
    rotary_width = cache_rope.shape[1]
    positions = cache_latent.shape[1]
    rotary = query_rope.reshape(count, heads, rotary_width)
    scores = jnp.einsum(
        "rhl,rpl->rhp", query_latent, cache_latent, preferred_element_type=jnp.float32
    )
    scores = scores + jnp.einsum(
        "rhe,rep->rhp", rotary, cache_rope, preferred_element_type=jnp.float32
    )
    scores = scores * score_scale
    valid = jnp.arange(positions, dtype=jnp.int32)[None, None, :] < cache_len[:, None, None]
    scores = jnp.where(valid, scores, -1e30)
    highest = jnp.max(scores, axis=-1, keepdims=True)
    powers = jnp.exp(scores - highest)
    weights = (powers / jnp.sum(powers, axis=-1, keepdims=True)).astype(jnp.bfloat16)
    mixed = jnp.einsum("rhp,rpl->rhl", weights, cache_latent, preferred_element_type=jnp.float32)
    return mixed.astype(jnp.bfloat16)


def split3(v):
    high = v.astype(jnp.bfloat16)
    rest = v - high.astype(jnp.float32)
    middle = rest.astype(jnp.bfloat16)
    low = (rest - middle.astype(jnp.float32)).astype(jnp.bfloat16)
    return high, middle, low


vmem_params = pltpu.CompilerParams(vmem_limit_bytes=40 * 1024 * 1024)
whole = pl.BlockSpec(memory_space=pltpu.VMEM)


def pack_kernel(shares, experts, routes_ref, rows_ref, out_ref):
    f32, bf16 = jnp.float32, jnp.bfloat16
    rows, width = rows_ref.shape
    part = width // shares
    chunk = shares * CAP
    lane = lax.broadcasted_iota(jnp.int32, (rows, experts * chunk), 1)
    expert, slot, quarter = lane // chunk, lane % CAP, lane % chunk // CAP
    named = jnp.zeros(lane.shape, f32)
    for k in range(routes_ref.shape[1]):
        named = jnp.where(routes_ref[:, k : k + 1] == expert, 1.0, named)
    before = lax.broadcasted_iota(jnp.int32, (rows, rows), 0) > lax.broadcasted_iota(
        jnp.int32, (rows, rows), 1
    )
    earlier = jnp.dot(before.astype(f32), named, preferred_element_type=f32)
    taken = jnp.where(earlier == slot.astype(f32), named, 0.0)
    select = jnp.concatenate(
        [jnp.where(quarter == q, taken, 0.0) for q in range(shares)], axis=0
    )
    values = rows_ref[...].astype(f32)
    values = jnp.concatenate(
        [values[:, q * part : (q + 1) * part] for q in range(shares)], axis=0
    )
    out_ref[...] = jnp.dot(
        select.T.astype(bf16), values.astype(bf16), preferred_element_type=f32
    ).astype(bf16)


def pack_rows(routes, rows, shares, experts):
    part = rows.shape[1] // shares
    total = experts * shares * CAP
    return pl.pallas_call(
        functools.partial(pack_kernel, shares, experts),
        out_shape=jax.ShapeDtypeStruct((total, part), rows.dtype),
        in_specs=[whole] * 2,
        out_specs=whole,
        compiler_params=pltpu.CompilerParams(vmem_limit_bytes=58 * 1024 * 1024),
        cost_estimate=pl.CostEstimate(
            flops=2 * total * part * rows.shape[0] * shares,
            bytes_accessed=2 * total * part,
            transcendentals=0,
        ),
    )(routes, rows)


def hidden_kernel(count, shares, *refs):
    halves, (order_ref, gate_ref, up_ref, out_ref, wide) = refs[:count], refs[count:]
    rows, part = halves[0].shape
    slots = rows // shares
    for h in range(count):
        ordered = jnp.dot(
            order_ref[...], halves[h][...], preferred_element_type=jnp.float32
        ).astype(wide.dtype)
        for q in range(shares):
            wide[pl.ds(h * slots, slots), pl.ds(q * part, part)] = ordered[
                q * slots : (q + 1) * slots
            ]
    gate = jnp.dot(wide[...], gate_ref[...], preferred_element_type=jnp.float32)
    upper = jnp.dot(wide[...], up_ref[...], preferred_element_type=jnp.float32)
    out_ref[...] = (gate / (1.0 + jnp.exp(-gate)) * upper).astype(out_ref.dtype)


def hidden_units(halves, order, w_gate, w_up):
    count = len(halves)
    rows, part = halves[0].shape
    width, units = w_gate.shape
    shares = width // part
    total = count * rows // shares
    return pl.pallas_call(
        functools.partial(hidden_kernel, count, shares),
        out_shape=jax.ShapeDtypeStruct((total, units), jnp.bfloat16),
        in_specs=[whole] * (count + 3),
        out_specs=whole,
        scratch_shapes=[pltpu.VMEM((total, width), jnp.bfloat16)],
        compiler_params=vmem_params,
        cost_estimate=pl.CostEstimate(
            flops=4 * total * width * units,
            bytes_accessed=4 * width * units + 2 * total * width,
            transcendentals=total * units,
        ),
    )(*halves, order, w_gate, w_up)


def stack_kernel(shares, *refs):
    weights, out_ref = refs[:shares], refs[shares]
    units = out_ref.shape[0] // shares
    for s in range(shares):
        out_ref[pl.ds(s * units, units), :] = weights[s][pl.ds(0, units), :]


def stack_shares(weights, units):
    shares, part = len(weights), weights[0].shape[1]
    return pl.pallas_call(
        functools.partial(stack_kernel, shares),
        out_shape=jax.ShapeDtypeStruct((shares * units, part), jnp.bfloat16),
        in_specs=[whole] * shares,
        out_specs=whole,
        compiler_params=vmem_params,
        cost_estimate=pl.CostEstimate(
            flops=0, bytes_accessed=4 * shares * units * part, transcendentals=0
        ),
    )(*weights)


def down_early_kernel(shares, *refs):
    early, weights_ref, out_ref = refs[:shares], refs[shares], refs[shares + 1]
    slots = out_ref.shape[0] // shares
    count = early[0].shape[1]
    for block in range(shares):
        total = None
        for s in range(shares):
            of_sender = (block - s) % shares
            if of_sender == shares // 2:
                continue
            place = of_sender - (of_sender > shares // 2)
            units = early[s][pl.ds(place * slots, slots), :]
            weights = weights_ref[pl.ds(s * count, count), :]
            term = jnp.dot(units, weights, preferred_element_type=jnp.float32)
            total = term if total is None else total + term
        out_ref[pl.ds(block * slots, slots), :] = total


def down_late_kernel(shares, *refs):
    late, (weights_ref, early_ref, order_ref, out_ref, plain) = refs[:shares], refs[shares:]
    slots, count = late[0].shape
    half = slots // 2
    for block in range(shares):
        s = (block - shares // 2) % shares
        weights = weights_ref[pl.ds(s * count, count), :]
        term = jnp.dot(late[s][...], weights, preferred_element_type=jnp.float32)
        total = (early_ref[pl.ds(block * slots, slots), :] + term).astype(plain.dtype)
        plain[pl.ds(block * half, half), :] = total[:half]
        plain[pl.ds((shares + block) * half, half), :] = total[half:]
    for h in range(2):
        place = pl.ds(h * shares * half, shares * half)
        out_ref[place, :] = jnp.dot(
            order_ref[...], plain[place, :], preferred_element_type=jnp.float32
        ).astype(out_ref.dtype)


def down_early(early, weights):
    shares = len(early)
    units, part = early[0].shape[1], weights.shape[1]
    rows = early[0].shape[0] // (shares - 1) * shares
    return pl.pallas_call(
        functools.partial(down_early_kernel, shares),
        out_shape=jax.ShapeDtypeStruct((rows, part), jnp.float32),
        in_specs=[whole] * (shares + 1),
        out_specs=whole,
        compiler_params=vmem_params,
        cost_estimate=pl.CostEstimate(
            flops=2 * rows * part * (shares - 1) * units,
            bytes_accessed=4 * rows * part + 2 * units * part * shares,
            transcendentals=0,
        ),
    )(*early, weights)


def down_late(late, weights, early, order):
    shares = len(late)
    rows, part = early.shape
    return pl.pallas_call(
        functools.partial(down_late_kernel, shares),
        out_shape=jax.ShapeDtypeStruct((rows, part), jnp.bfloat16),
        in_specs=[whole] * (shares + 3),
        out_specs=whole,
        scratch_shapes=[pltpu.VMEM((rows, part), jnp.bfloat16)],
        compiler_params=vmem_params,
        cost_estimate=pl.CostEstimate(
            flops=2 * rows * part * (late[0].shape[1] + rows),
            bytes_accessed=6 * rows * part,
            transcendentals=0,
        ),
    )(*late, weights, early, order)


def place_kernel(shares, first_ref, *refs):
    pieces, out_ref = refs[:shares], refs[shares]
    part = pieces[0].shape[1]
    for d in range(shares):
        quarter = lax.rem(first_ref[0] + d, shares)
        place = pl.ds(pl.multiple_of(quarter * part, 128), part)
        out_ref[:, place] = pieces[d][...]


def place_quarters(first, pieces):
    shares = len(pieces)
    rows, part = pieces[0].shape
    return pl.pallas_call(
        functools.partial(place_kernel, shares),
        out_shape=jax.ShapeDtypeStruct((rows, shares * part), pieces[0].dtype),
        in_specs=[pl.BlockSpec(memory_space=pltpu.SMEM)] + [whole] * shares,
        out_specs=whole,
        compiler_params=vmem_params,
        cost_estimate=pl.CostEstimate(
            flops=0, bytes_accessed=4 * rows * shares * part, transcendentals=0
        ),
    )(first.reshape(1), *pieces)


def gates_kernel(shares, chosen, *refs):
    f32 = jnp.float32
    infos, out_ref = refs[:shares], refs[shares]
    rows = out_ref.shape[0] // (3 * shares)
    lane = lax.broadcasted_iota(jnp.int32, (rows, out_ref.shape[1]), 1)
    chunk = shares * CAP
    expert, slot, block = lane // chunk, lane % CAP, lane % chunk // CAP
    expert, slot = expert.astype(f32), slot.astype(f32)
    before = lax.broadcasted_iota(jnp.int32, (rows, rows), 0) > lax.broadcasted_iota(
        jnp.int32, (rows, rows), 1
    )
    parts = []
    for d in range(shares):
        info = infos[d][...].astype(f32)[:rows]
        named = jnp.zeros(lane.shape, f32)
        gate = jnp.zeros(lane.shape, f32)
        for k in range(chosen):
            here = info[:, k : k + 1] == expert
            value = (info[:, chosen + k : chosen + k + 1] + info[:, 2 * chosen + k : 2 * chosen + k + 1]) + info[
                :, 3 * chosen + k : 3 * chosen + k + 1
            ]
            named = jnp.where(here, 1.0, named)
            gate = jnp.where(here, value, gate)
        earlier = jnp.dot(before.astype(f32), named, preferred_element_type=f32)
        taken = (earlier == slot) & (block == d)
        parts.append(jnp.where(taken, gate, 0.0))
    out_ref[...] = jnp.concatenate(split3(jnp.concatenate(parts, axis=0)), axis=0)


def gates_of_slots(infos, units, rows, chosen, experts):
    shares = len(infos)
    slots = experts * shares * CAP
    below = pl.BlockSpec((INFO, 128), lambda n: (units // INFO, 0))
    return pl.pallas_call(
        functools.partial(gates_kernel, shares, chosen),
        grid=(1,),
        out_shape=jax.ShapeDtypeStruct((3 * shares * rows, slots), jnp.bfloat16),
        in_specs=[below] * shares,
        out_specs=pl.BlockSpec((3 * shares * rows, slots), lambda n: (0, 0)),
        compiler_params=vmem_params,
        cost_estimate=pl.CostEstimate(flops=0, bytes_accessed=6 * shares * rows * slots, transcendentals=0),
    )(*infos)


def combine_kernel(shares, gates_ref, values_ref, *outs):
    sums = jnp.dot(gates_ref[...], values_ref[...], preferred_element_type=jnp.float32)
    count = sums.shape[0] // 3
    sums = sums[2 * count :] + sums[count : 2 * count] + sums[:count]
    rows = count // shares
    for d in range(shares):
        outs[d][...] = sums[d * rows : (d + 1) * rows].astype(outs[d].dtype)


def combine_slots(gates, values, shares):
    rows, part = gates.shape[0] // (3 * shares), values.shape[1]
    return pl.pallas_call(
        functools.partial(combine_kernel, shares),
        out_shape=(jax.ShapeDtypeStruct((rows, part), jnp.bfloat16),) * shares,
        in_specs=[whole] * 2,
        out_specs=(whole,) * shares,
        compiler_params=vmem_params,
        cost_estimate=pl.CostEstimate(
            flops=2 * gates.size * part, bytes_accessed=2 * values.size, transcendentals=0
        ),
    )(gates, values)


def per_device(
    query_latent,
    query_rope,
    cache_latent,
    cache_rope,
    cache_len,
    moe_input,
    routes,
    gate_weights,
    w_gate,
    w_up,
    w_down,
):
    bf16, f32 = jnp.bfloat16, jnp.float32
    shares = lax.axis_size("tensor")
    experts = lax.axis_size("expert")
    me = lax.axis_index("tensor")
    rows, width = moe_input.shape
    chosen = routes.shape[1]
    units = w_gate.shape[2]
    part = width // shares
    slots = experts * CAP

    def shift(value, by):
        pairs = [(i, (i + by) % shares) for i in range(shares)]
        return lax.ppermute(value, "tensor", pairs)

    packed = pack_rows(routes, moe_input, shares, experts)
    packed, w_down, routes, gate_weights = lax.optimization_barrier(
        (packed, w_down, routes, gate_weights)
    )
    received = lax.all_to_all(
        packed.reshape(experts, shares * CAP, part),
        "expert",
        split_axis=0,
        concat_axis=0,
        tiled=True,
    ).reshape(shares * slots, part)
    info = jnp.concatenate((routes.astype(bf16),) + split3(gate_weights), axis=1)
    info = jnp.pad(info, ((0, INFO - rows), (0, part - info.shape[1])))
    down_parts = [
        jnp.concatenate(
            [
                lax.dynamic_slice(w_down[0], (0, ((me + by) % shares) * part), (units, part)),
                info,
            ],
            axis=0,
        )
        for by in range(shares)
    ]
    down = [down_parts[0]] + [shift(down_parts[by], by) for by in range(1, shares)]
    local_context = attend(query_latent, query_rope, cache_latent, cache_rope, cache_len)
    heads, latent = local_context.shape[1:]
    received, local_context = lax.optimization_barrier((received, local_context))

    half = shares * slots // 2
    low, high = received[:half], received[half:]
    place = jnp.arange(half, dtype=jnp.int32)
    by_quarter = place // (half // shares), place % (half // shares)
    source = by_quarter[1] // CAP * (shares * CAP) + by_quarter[0] * CAP + by_quarter[1] % CAP
    sort = (source[:, None] == place[None, :]).astype(bf16)

    def hidden_of(*halves):
        return hidden_units(halves, sort, w_gate[0], w_up[0])

    low1, high3 = shift(low, 1), shift(high, 3)
    hidden0 = hidden_of(low, high)
    low, high, hidden0, down = lax.optimization_barrier((low, high, hidden0, down))
    high1, low3 = shift(high, 1), shift(low, 3)
    low2, high2 = shift(low1, 1), shift(high3, 3)
    hidden13 = hidden_of(low1, high1, low3, high3)
    hidden13, down = lax.optimization_barrier((hidden13, down))
    stacked = stack_shares(down, units)
    early = jnp.concatenate([hidden0, hidden13], axis=0)
    early = [early] + [shift(early, by) for by in range(1, shares)]
    late = hidden_of(low2, high2)
    late = [late] + [shift(late, by) for by in range(1, shares)]

    expert_out = down_late(late, stacked, down_early(early, stacked), sort.T)
    expert_out, local_context, down = lax.optimization_barrier(
        (expert_out, local_context, down)
    )

    returned = lax.all_to_all(
        expert_out.reshape(experts, shares * CAP, part),
        "expert",
        split_axis=0,
        concat_axis=0,
        tiled=True,
    ).reshape(experts * shares * CAP, part)
    context_parts = [
        lax.dynamic_slice(
            local_context, (((me + by) % shares) * rows, 0, 0), (rows, heads, latent)
        )
        for by in range(shares)
    ]
    context_parts = [context_parts[0]] + [
        shift(context_parts[by], by) for by in range(1, shares)
    ]

    context = jnp.zeros((rows, shares, heads, latent), bf16)
    for by in range(shares):
        context = lax.dynamic_update_slice(
            context, context_parts[by][:, None], (0, (me - by) % shares, 0, 0)
        )

    combine = gates_of_slots(down, units, rows, chosen, experts)
    returned, context, combine = lax.optimization_barrier((returned, context, combine))
    sums = combine_slots(combine, returned, shares)
    pieces = [sums[0]] + [shift(sums[d], shares - d) for d in range(1, shares)]
    moe_output = place_quarters(me, pieces)
    return (context.reshape(rows, shares * heads, latent), moe_output)


def solution(mesh):
    return jax.shard_map(
        per_device,
        mesh=mesh,
        in_specs=(
            P("expert", "tensor", None),
            P("expert", "tensor"),
            P("expert", None, None),
            P("expert", None, None),
            P("expert"),
            P(("expert", "tensor"), None),
            P(("expert", "tensor"), None),
            P(("expert", "tensor"), None),
            P("expert", None, "tensor"),
            P("expert", None, "tensor"),
            P("expert", "tensor", None),
        ),
        out_specs=(P(("expert", "tensor"), None, None), P(("expert", "tensor"), None)),
        check_vma=False,
    )
```

```python
import functools

import jax
import jax.numpy as jnp
from jax import lax
from jax.experimental import pallas as pl
from jax.experimental.pallas import tpu as pltpu
from jax.sharding import PartitionSpec as P

score_scale = 192.0 ** (-0.5)
CAP = 2
INFO = 16


def attend(query_latent, query_rope, cache_latent, cache_rope, cache_len):
    count, heads, latent = query_latent.shape
    rotary_width = cache_rope.shape[1]
    positions = cache_latent.shape[1]
    rotary = query_rope.reshape(count, heads, rotary_width)
    scores = jnp.einsum(
        "rhl,rpl->rhp", query_latent, cache_latent, preferred_element_type=jnp.float32
    )
    scores = scores + jnp.einsum(
        "rhe,rep->rhp", rotary, cache_rope, preferred_element_type=jnp.float32
    )
    scores = scores * score_scale
    valid = jnp.arange(positions, dtype=jnp.int32)[None, None, :] < cache_len[:, None, None]
    scores = jnp.where(valid, scores, -1e30)
    highest = jnp.max(scores, axis=-1, keepdims=True)
    powers = jnp.exp(scores - highest)
    weights = (powers / jnp.sum(powers, axis=-1, keepdims=True)).astype(jnp.bfloat16)
    mixed = jnp.einsum("rhp,rpl->rhl", weights, cache_latent, preferred_element_type=jnp.float32)
    return mixed.astype(jnp.bfloat16)


def far_order(shares):
    return [0] + sorted(range(1, shares), key=lambda by: -min(by, shares - by))


def arranged(values):
    return [values[by] for by in far_order(len(values))]


def restored(values):
    order = far_order(len(values))
    return [values[order.index(by)] for by in range(len(values))]


def split3(v):
    high = v.astype(jnp.bfloat16)
    rest = v - high.astype(jnp.float32)
    middle = rest.astype(jnp.bfloat16)
    low = (rest - middle.astype(jnp.float32)).astype(jnp.bfloat16)
    return high, middle, low


vmem_params = pltpu.CompilerParams(vmem_limit_bytes=40 * 1024 * 1024)
whole = pl.BlockSpec(memory_space=pltpu.VMEM)


def pack_kernel(shares, experts, routes_ref, rows_ref, out_ref):
    f32, bf16 = jnp.float32, jnp.bfloat16
    rows, width = rows_ref.shape
    part = width // shares
    chunk = shares * CAP
    lane = lax.broadcasted_iota(jnp.int32, (rows, experts * chunk), 1)
    expert, slot, quarter = lane // chunk, lane % CAP, lane % chunk // CAP
    named = jnp.zeros(lane.shape, f32)
    for k in range(routes_ref.shape[1]):
        named = jnp.where(routes_ref[:, k : k + 1] == expert, 1.0, named)
    before = lax.broadcasted_iota(jnp.int32, (rows, rows), 0) > lax.broadcasted_iota(
        jnp.int32, (rows, rows), 1
    )
    earlier = jnp.dot(before.astype(f32), named, preferred_element_type=f32)
    taken = jnp.where(earlier == slot.astype(f32), named, 0.0)
    select = jnp.concatenate(
        [jnp.where(quarter == q, taken, 0.0) for q in range(shares)], axis=0
    )
    values = rows_ref[...].astype(f32)
    values = jnp.concatenate(
        [values[:, q * part : (q + 1) * part] for q in range(shares)], axis=0
    )
    out_ref[...] = jnp.dot(
        select.T.astype(bf16), values.astype(bf16), preferred_element_type=f32
    ).astype(bf16)


def pack_rows(routes, rows, shares, experts):
    part = rows.shape[1] // shares
    total = experts * shares * CAP
    return pl.pallas_call(
        functools.partial(pack_kernel, shares, experts),
        out_shape=jax.ShapeDtypeStruct((total, part), rows.dtype),
        in_specs=[whole] * 2,
        out_specs=whole,
        compiler_params=pltpu.CompilerParams(vmem_limit_bytes=58 * 1024 * 1024),
        cost_estimate=pl.CostEstimate(
            flops=2 * total * part * rows.shape[0] * shares,
            bytes_accessed=2 * total * part,
            transcendentals=0,
        ),
    )(routes, rows)


def hidden_kernel(count, shares, *refs):
    halves, (order_ref, gate_ref, up_ref, out_ref, wide) = refs[:count], refs[count:]
    rows, part = halves[0].shape
    slots = rows // shares
    for h in range(count):
        ordered = jnp.dot(
            order_ref[...], halves[h][...], preferred_element_type=jnp.float32
        ).astype(wide.dtype)
        for q in range(shares):
            wide[pl.ds(h * slots, slots), pl.ds(q * part, part)] = ordered[
                q * slots : (q + 1) * slots
            ]
    gate = jnp.dot(wide[...], gate_ref[...], preferred_element_type=jnp.float32)
    upper = jnp.dot(wide[...], up_ref[...], preferred_element_type=jnp.float32)
    out_ref[...] = (gate / (1.0 + jnp.exp(-gate)) * upper).astype(out_ref.dtype)


def hidden_units(halves, order, w_gate, w_up):
    count = len(halves)
    rows, part = halves[0].shape
    width, units = w_gate.shape
    shares = width // part
    total = count * rows // shares
    return pl.pallas_call(
        functools.partial(hidden_kernel, count, shares),
        out_shape=jax.ShapeDtypeStruct((total, units), jnp.bfloat16),
        in_specs=[whole] * (count + 3),
        out_specs=whole,
        scratch_shapes=[pltpu.VMEM((total, width), jnp.bfloat16)],
        compiler_params=vmem_params,
        cost_estimate=pl.CostEstimate(
            flops=4 * total * width * units,
            bytes_accessed=4 * width * units + 2 * total * width,
            transcendentals=total * units,
        ),
    )(*halves, order, w_gate, w_up)


def stack_kernel(shares, *refs):
    weights, out_ref = restored(refs[:shares]), refs[shares]
    units = out_ref.shape[0] // shares
    for s in range(shares):
        out_ref[pl.ds(s * units, units), :] = weights[s][pl.ds(0, units), :]


def stack_shares(weights, units):
    shares, part = len(weights), weights[0].shape[1]
    return pl.pallas_call(
        functools.partial(stack_kernel, shares),
        out_shape=jax.ShapeDtypeStruct((shares * units, part), jnp.bfloat16),
        in_specs=[whole] * shares,
        out_specs=whole,
        compiler_params=vmem_params,
        cost_estimate=pl.CostEstimate(
            flops=0, bytes_accessed=4 * shares * units * part, transcendentals=0
        ),
    )(*arranged(weights))


def down_early_kernel(shares, *refs):
    early, weights_ref, out_ref = restored(refs[:shares]), refs[shares], refs[shares + 1]
    slots = out_ref.shape[0] // shares
    count = early[0].shape[1]
    for block in range(shares):
        total = None
        for s in range(shares):
            of_sender = (block - s) % shares
            if of_sender == shares // 2:
                continue
            place = of_sender - (of_sender > shares // 2)
            units = early[s][pl.ds(place * slots, slots), :]
            weights = weights_ref[pl.ds(s * count, count), :]
            term = jnp.dot(units, weights, preferred_element_type=jnp.float32)
            total = term if total is None else total + term
        out_ref[pl.ds(block * slots, slots), :] = total


def down_late_kernel(shares, *refs):
    late = restored(refs[:shares])
    weights_ref, early_ref, order_ref, out_ref, plain = refs[shares:]
    slots, count = late[0].shape
    half = slots // 2
    for block in range(shares):
        s = (block - shares // 2) % shares
        weights = weights_ref[pl.ds(s * count, count), :]
        term = jnp.dot(late[s][...], weights, preferred_element_type=jnp.float32)
        total = (early_ref[pl.ds(block * slots, slots), :] + term).astype(plain.dtype)
        plain[pl.ds(block * half, half), :] = total[:half]
        plain[pl.ds((shares + block) * half, half), :] = total[half:]
    for h in range(2):
        place = pl.ds(h * shares * half, shares * half)
        out_ref[place, :] = jnp.dot(
            order_ref[...], plain[place, :], preferred_element_type=jnp.float32
        ).astype(out_ref.dtype)


def down_early(early, weights):
    shares = len(early)
    units, part = early[0].shape[1], weights.shape[1]
    rows = early[0].shape[0] // (shares - 1) * shares
    return pl.pallas_call(
        functools.partial(down_early_kernel, shares),
        out_shape=jax.ShapeDtypeStruct((rows, part), jnp.float32),
        in_specs=[whole] * (shares + 1),
        out_specs=whole,
        compiler_params=vmem_params,
        cost_estimate=pl.CostEstimate(
            flops=2 * rows * part * (shares - 1) * units,
            bytes_accessed=4 * rows * part + 2 * units * part * shares,
            transcendentals=0,
        ),
    )(*arranged(early), weights)


def down_late(late, weights, early, order):
    shares = len(late)
    rows, part = early.shape
    return pl.pallas_call(
        functools.partial(down_late_kernel, shares),
        out_shape=jax.ShapeDtypeStruct((rows, part), jnp.bfloat16),
        in_specs=[whole] * (shares + 3),
        out_specs=whole,
        scratch_shapes=[pltpu.VMEM((rows, part), jnp.bfloat16)],
        compiler_params=vmem_params,
        cost_estimate=pl.CostEstimate(
            flops=2 * rows * part * (late[0].shape[1] + rows),
            bytes_accessed=6 * rows * part,
            transcendentals=0,
        ),
    )(*arranged(late), weights, early, order)


def place_kernel(shares, first_ref, *refs):
    pieces, out_ref = restored(refs[:shares]), refs[shares]
    part = pieces[0].shape[1]
    for d in range(shares):
        quarter = lax.rem(first_ref[0] + d, shares)
        place = pl.ds(pl.multiple_of(quarter * part, 128), part)
        out_ref[:, place] = pieces[d][...]


def place_quarters(first, pieces):
    shares = len(pieces)
    rows, part = pieces[0].shape
    return pl.pallas_call(
        functools.partial(place_kernel, shares),
        out_shape=jax.ShapeDtypeStruct((rows, shares * part), pieces[0].dtype),
        in_specs=[pl.BlockSpec(memory_space=pltpu.SMEM)] + [whole] * shares,
        out_specs=whole,
        compiler_params=vmem_params,
        cost_estimate=pl.CostEstimate(
            flops=0, bytes_accessed=4 * rows * shares * part, transcendentals=0
        ),
    )(first.reshape(1), *arranged(pieces))


def gates_kernel(shares, chosen, *refs):
    f32 = jnp.float32
    infos, out_ref = refs[:shares], refs[shares]
    rows = out_ref.shape[0] // (3 * shares)
    lane = lax.broadcasted_iota(jnp.int32, (rows, out_ref.shape[1]), 1)
    chunk = shares * CAP
    expert, slot, block = lane // chunk, lane % CAP, lane % chunk // CAP
    expert, slot = expert.astype(f32), slot.astype(f32)
    before = lax.broadcasted_iota(jnp.int32, (rows, rows), 0) > lax.broadcasted_iota(
        jnp.int32, (rows, rows), 1
    )
    parts = []
    for d in range(shares):
        info = infos[d][...].astype(f32)[:rows]
        named = jnp.zeros(lane.shape, f32)
        gate = jnp.zeros(lane.shape, f32)
        for k in range(chosen):
            here = info[:, k : k + 1] == expert
            value = (info[:, chosen + k : chosen + k + 1] + info[:, 2 * chosen + k : 2 * chosen + k + 1]) + info[
                :, 3 * chosen + k : 3 * chosen + k + 1
            ]
            named = jnp.where(here, 1.0, named)
            gate = jnp.where(here, value, gate)
        earlier = jnp.dot(before.astype(f32), named, preferred_element_type=f32)
        taken = (earlier == slot) & (block == d)
        parts.append(jnp.where(taken, gate, 0.0))
    out_ref[...] = jnp.concatenate(split3(jnp.concatenate(parts, axis=0)), axis=0)


def gates_of_slots(infos, units, rows, chosen, experts):
    shares = len(infos)
    slots = experts * shares * CAP
    below = pl.BlockSpec((INFO, 128), lambda n: (units // INFO, 0))
    return pl.pallas_call(
        functools.partial(gates_kernel, shares, chosen),
        grid=(1,),
        out_shape=jax.ShapeDtypeStruct((3 * shares * rows, slots), jnp.bfloat16),
        in_specs=[below] * shares,
        out_specs=pl.BlockSpec((3 * shares * rows, slots), lambda n: (0, 0)),
        compiler_params=vmem_params,
        cost_estimate=pl.CostEstimate(flops=0, bytes_accessed=6 * shares * rows * slots, transcendentals=0),
    )(*infos)


def combine_kernel(shares, gates_ref, values_ref, *outs):
    sums = jnp.dot(gates_ref[...], values_ref[...], preferred_element_type=jnp.float32)
    count = sums.shape[0] // 3
    sums = sums[2 * count :] + sums[count : 2 * count] + sums[:count]
    rows = count // shares
    for d in range(shares):
        outs[d][...] = sums[d * rows : (d + 1) * rows].astype(outs[d].dtype)


def combine_slots(gates, values, shares):
    rows, part = gates.shape[0] // (3 * shares), values.shape[1]
    return pl.pallas_call(
        functools.partial(combine_kernel, shares),
        out_shape=(jax.ShapeDtypeStruct((rows, part), jnp.bfloat16),) * shares,
        in_specs=[whole] * 2,
        out_specs=(whole,) * shares,
        compiler_params=vmem_params,
        cost_estimate=pl.CostEstimate(
            flops=2 * gates.size * part, bytes_accessed=2 * values.size, transcendentals=0
        ),
    )(gates, values)


def per_device(
    query_latent,
    query_rope,
    cache_latent,
    cache_rope,
    cache_len,
    moe_input,
    routes,
    gate_weights,
    w_gate,
    w_up,
    w_down,
):
    bf16, f32 = jnp.bfloat16, jnp.float32
    shares = lax.axis_size("tensor")
    experts = lax.axis_size("expert")
    me = lax.axis_index("tensor")
    rows, width = moe_input.shape
    chosen = routes.shape[1]
    units = w_gate.shape[2]
    part = width // shares
    slots = experts * CAP

    def shift(value, by):
        pairs = [(i, (i + by) % shares) for i in range(shares)]
        return lax.ppermute(value, "tensor", pairs)

    def spread(values):
        moved = {by: shift(values[by], by) for by in far_order(shares)[1:]}
        return [values[0]] + [moved[by] for by in range(1, shares)]

    packed = pack_rows(routes, moe_input, shares, experts)
    packed, w_down, routes, gate_weights = lax.optimization_barrier(
        (packed, w_down, routes, gate_weights)
    )
    received = lax.all_to_all(
        packed.reshape(experts, shares * CAP, part),
        "expert",
        split_axis=0,
        concat_axis=0,
        tiled=True,
    ).reshape(shares * slots, part)
    info = jnp.concatenate((routes.astype(bf16),) + split3(gate_weights), axis=1)
    info = jnp.pad(info, ((0, INFO - rows), (0, part - info.shape[1])))
    down_parts = [
        jnp.concatenate(
            [
                lax.dynamic_slice(w_down[0], (0, ((me + by) % shares) * part), (units, part)),
                info,
            ],
            axis=0,
        )
        for by in range(shares)
    ]
    down = spread(down_parts)
    local_context = attend(query_latent, query_rope, cache_latent, cache_rope, cache_len)
    heads, latent = local_context.shape[1:]
    received, local_context = lax.optimization_barrier((received, local_context))

    half = shares * slots // 2
    low, high = received[:half], received[half:]
    place = jnp.arange(half, dtype=jnp.int32)
    by_quarter = place // (half // shares), place % (half // shares)
    source = by_quarter[1] // CAP * (shares * CAP) + by_quarter[0] * CAP + by_quarter[1] % CAP
    sort = (source[:, None] == place[None, :]).astype(bf16)

    def hidden_of(*halves):
        return hidden_units(halves, sort, w_gate[0], w_up[0])

    low1, high3 = shift(low, 1), shift(high, 3)
    hidden0 = hidden_of(low, high)
    low, high, hidden0, down = lax.optimization_barrier((low, high, hidden0, arranged(down)))
    high1, low3 = shift(high, 1), shift(low, 3)
    low2, high2 = shift(low1, 1), shift(high3, 3)
    hidden13 = hidden_of(low1, high1, low3, high3)
    hidden13, down = lax.optimization_barrier((hidden13, down))
    down = restored(down)
    stacked = stack_shares(down, units)
    early = jnp.concatenate([hidden0, hidden13], axis=0)
    early = spread([early] * shares)
    late = hidden_of(low2, high2)
    late = spread([late] * shares)

    expert_out = down_late(late, stacked, down_early(early, stacked), sort.T)
    expert_out, local_context, down = lax.optimization_barrier(
        (expert_out, local_context, down)
    )

    returned = lax.all_to_all(
        expert_out.reshape(experts, shares * CAP, part),
        "expert",
        split_axis=0,
        concat_axis=0,
        tiled=True,
    ).reshape(experts * shares * CAP, part)
    context_parts = [
        lax.dynamic_slice(
            local_context, (((me + by) % shares) * rows, 0, 0), (rows, heads, latent)
        )
        for by in range(shares)
    ]
    context_parts = spread(context_parts)

    context = jnp.zeros((rows, shares, heads, latent), bf16)
    for by in range(shares):
        context = lax.dynamic_update_slice(
            context, context_parts[by][:, None], (0, (me - by) % shares, 0, 0)
        )

    combine = gates_of_slots(down, units, rows, chosen, experts)
    returned, context, combine = lax.optimization_barrier((returned, context, combine))
    sums = combine_slots(combine, returned, shares)
    pieces = {by: shift(sums[shares - by], by) for by in far_order(shares)[1:]}
    pieces = [sums[0]] + [pieces[shares - d] for d in range(1, shares)]
    moe_output = place_quarters(me, pieces)
    return (context.reshape(rows, shares * heads, latent), moe_output)


def solution(mesh):
    return jax.shard_map(
        per_device,
        mesh=mesh,
        in_specs=(
            P("expert", "tensor", None),
            P("expert", "tensor"),
            P("expert", None, None),
            P("expert", None, None),
            P("expert"),
            P(("expert", "tensor"), None),
            P(("expert", "tensor"), None),
            P(("expert", "tensor"), None),
            P("expert", None, "tensor"),
            P("expert", None, "tensor"),
            P("expert", "tensor", None),
        ),
        out_specs=(P(("expert", "tensor"), None, None), P(("expert", "tensor"), None)),
        check_vma=False,
    )
```

```python
import functools

import jax
import jax.numpy as jnp
from jax import lax
from jax.experimental import pallas as pl
from jax.experimental.pallas import tpu as pltpu
from jax.sharding import PartitionSpec as P

score_scale = 192.0 ** (-0.5)
CAP = 2
INFO = 16


def attend(query_latent, query_rope, cache_latent, cache_rope, cache_len):
    count, heads, latent = query_latent.shape
    rotary_width = cache_rope.shape[1]
    positions = cache_latent.shape[1]
    rotary = query_rope.reshape(count, heads, rotary_width)
    scores = jnp.einsum(
        "rhl,rpl->rhp", query_latent, cache_latent, preferred_element_type=jnp.float32
    )
    scores = scores + jnp.einsum(
        "rhe,rep->rhp", rotary, cache_rope, preferred_element_type=jnp.float32
    )
    scores = scores * score_scale
    valid = jnp.arange(positions, dtype=jnp.int32)[None, None, :] < cache_len[:, None, None]
    scores = jnp.where(valid, scores, -1e30)
    highest = jnp.max(scores, axis=-1, keepdims=True)
    powers = jnp.exp(scores - highest)
    weights = (powers / jnp.sum(powers, axis=-1, keepdims=True)).astype(jnp.bfloat16)
    mixed = jnp.einsum("rhp,rpl->rhl", weights, cache_latent, preferred_element_type=jnp.float32)
    return mixed.astype(jnp.bfloat16)


def split3(v):
    high = v.astype(jnp.bfloat16)
    rest = v - high.astype(jnp.float32)
    middle = rest.astype(jnp.bfloat16)
    low = (rest - middle.astype(jnp.float32)).astype(jnp.bfloat16)
    return high, middle, low


vmem_params = pltpu.CompilerParams(vmem_limit_bytes=40 * 1024 * 1024)
whole = pl.BlockSpec(memory_space=pltpu.VMEM)


def pack_kernel(shares, experts, routes_ref, rows_ref, out_ref, held, sems):
    f32, bf16 = jnp.float32, jnp.bfloat16
    rows, width = rows_ref.shape
    part = width // shares
    chunk = shares * CAP
    lane = lax.broadcasted_iota(jnp.int32, (rows, experts * chunk), 1)
    expert, slot, quarter = lane // chunk, lane % CAP, lane % chunk // CAP
    named = jnp.zeros(lane.shape, f32)
    for k in range(routes_ref.shape[1]):
        named = jnp.where(routes_ref[:, k : k + 1] == expert, 1.0, named)
    before = lax.broadcasted_iota(jnp.int32, (rows, rows), 0) > lax.broadcasted_iota(
        jnp.int32, (rows, rows), 1
    )
    earlier = jnp.dot(before.astype(f32), named, preferred_element_type=f32)
    taken = jnp.where(earlier == slot.astype(f32), named, 0.0)
    select = jnp.concatenate(
        [jnp.where(quarter == q, taken, 0.0) for q in range(shares)], axis=0
    )
    values = rows_ref[...].astype(f32)
    values = jnp.concatenate(
        [values[:, q * part : (q + 1) * part] for q in range(shares)], axis=0
    )
    select, values = select.T.astype(bf16), values.astype(bf16)
    step = held.shape[0] // sems.shape[0]
    copies = []
    for n in range(sems.shape[0]):
        place = pl.ds(n * step, step)
        held[place, :] = jnp.dot(
            select[n * step : (n + 1) * step], values, preferred_element_type=f32
        ).astype(bf16)
        copies.append(pltpu.make_async_copy(held.at[place], out_ref.at[place], sems.at[n]))
        copies[-1].start()
    for copy in copies:
        copy.wait()


def pack_rows(routes, rows, shares, experts):
    part = rows.shape[1] // shares
    total = experts * shares * CAP
    return pl.pallas_call(
        functools.partial(pack_kernel, shares, experts),
        out_shape=jax.ShapeDtypeStruct((total, part), rows.dtype),
        in_specs=[whole] * 2,
        out_specs=pl.BlockSpec(memory_space=pl.ANY),
        scratch_shapes=[
            pltpu.VMEM((total, part), rows.dtype),
            pltpu.SemaphoreType.DMA((4,)),
        ],
        compiler_params=pltpu.CompilerParams(vmem_limit_bytes=58 * 1024 * 1024),
        cost_estimate=pl.CostEstimate(
            flops=2 * total * part * rows.shape[0] * shares,
            bytes_accessed=2 * total * part,
            transcendentals=0,
        ),
    )(routes, rows)


def hidden_kernel(count, shares, *refs):
    halves, (order_ref, gate_ref, up_ref, out_ref, wide) = refs[:count], refs[count:]
    rows, part = halves[0].shape
    slots = rows // shares
    for h in range(count):
        ordered = jnp.dot(
            order_ref[...], halves[h][...], preferred_element_type=jnp.float32
        ).astype(wide.dtype)
        for q in range(shares):
            wide[pl.ds(h * slots, slots), pl.ds(q * part, part)] = ordered[
                q * slots : (q + 1) * slots
            ]
    gate = jnp.dot(wide[...], gate_ref[...], preferred_element_type=jnp.float32)
    upper = jnp.dot(wide[...], up_ref[...], preferred_element_type=jnp.float32)
    out_ref[...] = (gate / (1.0 + jnp.exp(-gate)) * upper).astype(out_ref.dtype)


def hidden_units(halves, order, w_gate, w_up):
    count = len(halves)
    rows, part = halves[0].shape
    width, units = w_gate.shape
    shares = width // part
    total = count * rows // shares
    return pl.pallas_call(
        functools.partial(hidden_kernel, count, shares),
        out_shape=jax.ShapeDtypeStruct((total, units), jnp.bfloat16),
        in_specs=[whole] * (count + 3),
        out_specs=whole,
        scratch_shapes=[pltpu.VMEM((total, width), jnp.bfloat16)],
        compiler_params=vmem_params,
        cost_estimate=pl.CostEstimate(
            flops=4 * total * width * units,
            bytes_accessed=4 * width * units + 2 * total * width,
            transcendentals=total * units,
        ),
    )(*halves, order, w_gate, w_up)


def stack_kernel(shares, *refs):
    weights, out_ref = refs[:shares], refs[shares]
    units = out_ref.shape[0] // shares
    for s in range(shares):
        out_ref[pl.ds(s * units, units), :] = weights[s][pl.ds(0, units), :]


def stack_shares(weights, units):
    shares, part = len(weights), weights[0].shape[1]
    return pl.pallas_call(
        functools.partial(stack_kernel, shares),
        out_shape=jax.ShapeDtypeStruct((shares * units, part), jnp.bfloat16),
        in_specs=[whole] * shares,
        out_specs=whole,
        compiler_params=vmem_params,
        cost_estimate=pl.CostEstimate(
            flops=0, bytes_accessed=4 * shares * units * part, transcendentals=0
        ),
    )(*weights)


def down_early_kernel(shares, *refs):
    early, weights_ref, out_ref = refs[:shares], refs[shares], refs[shares + 1]
    slots = out_ref.shape[0] // shares
    count = early[0].shape[1]
    for block in range(shares):
        total = None
        for s in range(shares):
            of_sender = (block - s) % shares
            if of_sender == shares // 2:
                continue
            place = of_sender - (of_sender > shares // 2)
            units = early[s][pl.ds(place * slots, slots), :]
            weights = weights_ref[pl.ds(s * count, count), :]
            term = jnp.dot(units, weights, preferred_element_type=jnp.float32)
            total = term if total is None else total + term
        out_ref[pl.ds(block * slots, slots), :] = total


def down_late_kernel(shares, *refs):
    late, (weights_ref, early_ref, order_ref, out_ref, plain, held, sems) = (
        refs[:shares],
        refs[shares:],
    )
    slots, count = late[0].shape
    half = slots // 2
    for block in range(shares):
        s = (block - shares // 2) % shares
        weights = weights_ref[pl.ds(s * count, count), :]
        term = jnp.dot(late[s][...], weights, preferred_element_type=jnp.float32)
        total = (early_ref[pl.ds(block * slots, slots), :] + term).astype(plain.dtype)
        plain[pl.ds(block * half, half), :] = total[:half]
        plain[pl.ds((shares + block) * half, half), :] = total[half:]
    copies = []
    for h in range(2):
        place = pl.ds(h * shares * half, shares * half)
        held[place, :] = jnp.dot(
            order_ref[...], plain[place, :], preferred_element_type=jnp.float32
        ).astype(held.dtype)
        copies.append(pltpu.make_async_copy(held.at[place], out_ref.at[place], sems.at[h]))
        copies[-1].start()
    for copy in copies:
        copy.wait()


def down_early(early, weights):
    shares = len(early)
    units, part = early[0].shape[1], weights.shape[1]
    rows = early[0].shape[0] // (shares - 1) * shares
    return pl.pallas_call(
        functools.partial(down_early_kernel, shares),
        out_shape=jax.ShapeDtypeStruct((rows, part), jnp.float32),
        in_specs=[whole] * (shares + 1),
        out_specs=whole,
        compiler_params=vmem_params,
        cost_estimate=pl.CostEstimate(
            flops=2 * rows * part * (shares - 1) * units,
            bytes_accessed=4 * rows * part + 2 * units * part * shares,
            transcendentals=0,
        ),
    )(*early, weights)


def down_late(late, weights, early, order):
    shares = len(late)
    rows, part = early.shape
    return pl.pallas_call(
        functools.partial(down_late_kernel, shares),
        out_shape=jax.ShapeDtypeStruct((rows, part), jnp.bfloat16),
        in_specs=[whole] * (shares + 3),
        out_specs=pl.BlockSpec(memory_space=pl.ANY),
        scratch_shapes=[
            pltpu.VMEM((rows, part), jnp.bfloat16),
            pltpu.VMEM((rows, part), jnp.bfloat16),
            pltpu.SemaphoreType.DMA((2,)),
        ],
        compiler_params=vmem_params,
        cost_estimate=pl.CostEstimate(
            flops=2 * rows * part * (late[0].shape[1] + rows),
            bytes_accessed=6 * rows * part,
            transcendentals=0,
        ),
    )(*late, weights, early, order)


def place_kernel(shares, first_ref, *refs):
    pieces, out_ref = refs[:shares], refs[shares]
    part = pieces[0].shape[1]
    for d in range(shares):
        quarter = lax.rem(first_ref[0] + d, shares)
        place = pl.ds(pl.multiple_of(quarter * part, 128), part)
        out_ref[:, place] = pieces[d][...]


def place_quarters(first, pieces):
    shares = len(pieces)
    rows, part = pieces[0].shape
    return pl.pallas_call(
        functools.partial(place_kernel, shares),
        out_shape=jax.ShapeDtypeStruct((rows, shares * part), pieces[0].dtype),
        in_specs=[pl.BlockSpec(memory_space=pltpu.SMEM)] + [whole] * shares,
        out_specs=whole,
        compiler_params=vmem_params,
        cost_estimate=pl.CostEstimate(
            flops=0, bytes_accessed=4 * rows * shares * part, transcendentals=0
        ),
    )(first.reshape(1), *pieces)


def gates_kernel(shares, chosen, *refs):
    f32 = jnp.float32
    infos, out_ref = refs[:shares], refs[shares]
    rows = out_ref.shape[0] // (3 * shares)
    lane = lax.broadcasted_iota(jnp.int32, (rows, out_ref.shape[1]), 1)
    chunk = shares * CAP
    expert, slot, block = lane // chunk, lane % CAP, lane % chunk // CAP
    expert, slot = expert.astype(f32), slot.astype(f32)
    before = lax.broadcasted_iota(jnp.int32, (rows, rows), 0) > lax.broadcasted_iota(
        jnp.int32, (rows, rows), 1
    )
    parts = []
    for d in range(shares):
        info = infos[d][...].astype(f32)[:rows]
        named = jnp.zeros(lane.shape, f32)
        gate = jnp.zeros(lane.shape, f32)
        for k in range(chosen):
            here = info[:, k : k + 1] == expert
            value = (info[:, chosen + k : chosen + k + 1] + info[:, 2 * chosen + k : 2 * chosen + k + 1]) + info[
                :, 3 * chosen + k : 3 * chosen + k + 1
            ]
            named = jnp.where(here, 1.0, named)
            gate = jnp.where(here, value, gate)
        earlier = jnp.dot(before.astype(f32), named, preferred_element_type=f32)
        taken = (earlier == slot) & (block == d)
        parts.append(jnp.where(taken, gate, 0.0))
    out_ref[...] = jnp.concatenate(split3(jnp.concatenate(parts, axis=0)), axis=0)


def gates_of_slots(infos, units, rows, chosen, experts):
    shares = len(infos)
    slots = experts * shares * CAP
    below = pl.BlockSpec((INFO, 128), lambda n: (units // INFO, 0))
    return pl.pallas_call(
        functools.partial(gates_kernel, shares, chosen),
        grid=(1,),
        out_shape=jax.ShapeDtypeStruct((3 * shares * rows, slots), jnp.bfloat16),
        in_specs=[below] * shares,
        out_specs=pl.BlockSpec((3 * shares * rows, slots), lambda n: (0, 0)),
        compiler_params=vmem_params,
        cost_estimate=pl.CostEstimate(flops=0, bytes_accessed=6 * shares * rows * slots, transcendentals=0),
    )(*infos)


def combine_kernel(shares, gates_ref, values_ref, *outs):
    sums = jnp.dot(gates_ref[...], values_ref[...], preferred_element_type=jnp.float32)
    count = sums.shape[0] // 3
    sums = sums[2 * count :] + sums[count : 2 * count] + sums[:count]
    rows = count // shares
    for d in range(shares):
        outs[d][...] = sums[d * rows : (d + 1) * rows].astype(outs[d].dtype)


def combine_slots(gates, values, shares):
    rows, part = gates.shape[0] // (3 * shares), values.shape[1]
    return pl.pallas_call(
        functools.partial(combine_kernel, shares),
        out_shape=(jax.ShapeDtypeStruct((rows, part), jnp.bfloat16),) * shares,
        in_specs=[whole] * 2,
        out_specs=(whole,) * shares,
        compiler_params=vmem_params,
        cost_estimate=pl.CostEstimate(
            flops=2 * gates.size * part, bytes_accessed=2 * values.size, transcendentals=0
        ),
    )(gates, values)


def per_device(
    query_latent,
    query_rope,
    cache_latent,
    cache_rope,
    cache_len,
    moe_input,
    routes,
    gate_weights,
    w_gate,
    w_up,
    w_down,
):
    bf16, f32 = jnp.bfloat16, jnp.float32
    shares = lax.axis_size("tensor")
    experts = lax.axis_size("expert")
    me = lax.axis_index("tensor")
    rows, width = moe_input.shape
    chosen = routes.shape[1]
    units = w_gate.shape[2]
    part = width // shares
    slots = experts * CAP

    def shift(value, by):
        pairs = [(i, (i + by) % shares) for i in range(shares)]
        return lax.ppermute(value, "tensor", pairs)

    packed = pack_rows(routes, moe_input, shares, experts)
    packed, w_down, routes, gate_weights = lax.optimization_barrier(
        (packed, w_down, routes, gate_weights)
    )
    received = lax.all_to_all(
        packed.reshape(experts, shares * CAP, part),
        "expert",
        split_axis=0,
        concat_axis=0,
        tiled=True,
    ).reshape(shares * slots, part)
    info = jnp.concatenate((routes.astype(bf16),) + split3(gate_weights), axis=1)
    info = jnp.pad(info, ((0, INFO - rows), (0, part - info.shape[1])))
    down_parts = [
        jnp.concatenate(
            [
                lax.dynamic_slice(w_down[0], (0, ((me + by) % shares) * part), (units, part)),
                info,
            ],
            axis=0,
        )
        for by in range(shares)
    ]
    down = [down_parts[0]] + [shift(down_parts[by], by) for by in range(1, shares)]
    local_context = attend(query_latent, query_rope, cache_latent, cache_rope, cache_len)
    heads, latent = local_context.shape[1:]
    received, local_context = lax.optimization_barrier((received, local_context))

    half = shares * slots // 2
    low, high = received[:half], received[half:]
    place = jnp.arange(half, dtype=jnp.int32)
    by_quarter = place // (half // shares), place % (half // shares)
    source = by_quarter[1] // CAP * (shares * CAP) + by_quarter[0] * CAP + by_quarter[1] % CAP
    sort = (source[:, None] == place[None, :]).astype(bf16)

    def hidden_of(*halves):
        return hidden_units(halves, sort, w_gate[0], w_up[0])

    low1, high3 = shift(low, 1), shift(high, 3)
    hidden0 = hidden_of(low, high)
    low, high, hidden0, down = lax.optimization_barrier((low, high, hidden0, down))
    high1, low3 = shift(high, 1), shift(low, 3)
    low2, high2 = shift(low1, 1), shift(high3, 3)
    hidden13 = hidden_of(low1, high1, low3, high3)
    hidden13, down = lax.optimization_barrier((hidden13, down))
    stacked = stack_shares(down, units)
    early = jnp.concatenate([hidden0, hidden13], axis=0)
    early = [early] + [shift(early, by) for by in range(1, shares)]
    late = hidden_of(low2, high2)
    late = [late] + [shift(late, by) for by in range(1, shares)]

    expert_out = down_late(late, stacked, down_early(early, stacked), sort.T)
    expert_out, local_context, down = lax.optimization_barrier(
        (expert_out, local_context, down)
    )

    returned = lax.all_to_all(
        expert_out.reshape(experts, shares * CAP, part),
        "expert",
        split_axis=0,
        concat_axis=0,
        tiled=True,
    ).reshape(experts * shares * CAP, part)
    context_parts = [
        lax.dynamic_slice(
            local_context, (((me + by) % shares) * rows, 0, 0), (rows, heads, latent)
        )
        for by in range(shares)
    ]
    context_parts = [context_parts[0]] + [
        shift(context_parts[by], by) for by in range(1, shares)
    ]

    context = jnp.zeros((rows, shares, heads, latent), bf16)
    for by in range(shares):
        context = lax.dynamic_update_slice(
            context, context_parts[by][:, None], (0, (me - by) % shares, 0, 0)
        )

    combine = gates_of_slots(down, units, rows, chosen, experts)
    returned, context, combine = lax.optimization_barrier((returned, context, combine))
    sums = combine_slots(combine, returned, shares)
    pieces = [sums[0]] + [shift(sums[d], shares - d) for d in range(1, shares)]
    moe_output = place_quarters(me, pieces)
    return (context.reshape(rows, shares * heads, latent), moe_output)


def solution(mesh):
    return jax.shard_map(
        per_device,
        mesh=mesh,
        in_specs=(
            P("expert", "tensor", None),
            P("expert", "tensor"),
            P("expert", None, None),
            P("expert", None, None),
            P("expert"),
            P(("expert", "tensor"), None),
            P(("expert", "tensor"), None),
            P(("expert", "tensor"), None),
            P("expert", None, "tensor"),
            P("expert", None, "tensor"),
            P("expert", "tensor", None),
        ),
        out_specs=(P(("expert", "tensor"), None, None), P(("expert", "tensor"), None)),
        check_vma=False,
    )
```

```python
import functools

import jax
import jax.numpy as jnp
from jax import lax
from jax.experimental import pallas as pl
from jax.experimental.pallas import tpu as pltpu
from jax.sharding import PartitionSpec as P

score_scale = 192.0 ** (-0.5)
CAP = 2
INFO = 16


def attend(query_latent, query_rope, cache_latent, cache_rope, cache_len):
    count, heads, latent = query_latent.shape
    rotary_width = cache_rope.shape[1]
    positions = cache_latent.shape[1]
    rotary = query_rope.reshape(count, heads, rotary_width)
    scores = jnp.einsum(
        "rhl,rpl->rhp", query_latent, cache_latent, preferred_element_type=jnp.float32
    )
    scores = scores + jnp.einsum(
        "rhe,rep->rhp", rotary, cache_rope, preferred_element_type=jnp.float32
    )
    scores = scores * score_scale
    valid = jnp.arange(positions, dtype=jnp.int32)[None, None, :] < cache_len[:, None, None]
    scores = jnp.where(valid, scores, -1e30)
    highest = jnp.max(scores, axis=-1, keepdims=True)
    powers = jnp.exp(scores - highest)
    weights = (powers / jnp.sum(powers, axis=-1, keepdims=True)).astype(jnp.bfloat16)
    mixed = jnp.einsum("rhp,rpl->rhl", weights, cache_latent, preferred_element_type=jnp.float32)
    return mixed.astype(jnp.bfloat16)


def split3(v):
    high = v.astype(jnp.bfloat16)
    rest = v - high.astype(jnp.float32)
    middle = rest.astype(jnp.bfloat16)
    low = (rest - middle.astype(jnp.float32)).astype(jnp.bfloat16)
    return high, middle, low


vmem_params = pltpu.CompilerParams(vmem_limit_bytes=40 * 1024 * 1024)
whole = pl.BlockSpec(memory_space=pltpu.VMEM)


def pack_kernel(shares, experts, routes_ref, rows_ref, out_ref, held, sems):
    f32, bf16 = jnp.float32, jnp.bfloat16
    rows, width = rows_ref.shape
    part = width // shares
    chunk = shares * CAP
    lane = lax.broadcasted_iota(jnp.int32, (rows, experts * chunk), 1)
    expert, slot, quarter = lane // chunk, lane % CAP, lane % chunk // CAP
    named = jnp.zeros(lane.shape, f32)
    for k in range(routes_ref.shape[1]):
        named = jnp.where(routes_ref[:, k : k + 1] == expert, 1.0, named)
    before = lax.broadcasted_iota(jnp.int32, (rows, rows), 0) > lax.broadcasted_iota(
        jnp.int32, (rows, rows), 1
    )
    earlier = jnp.dot(before.astype(f32), named, preferred_element_type=f32)
    taken = jnp.where(earlier == slot.astype(f32), named, 0.0)
    select = jnp.concatenate(
        [jnp.where(quarter == q, taken, 0.0) for q in range(shares)], axis=0
    )
    values = rows_ref[...].astype(f32)
    values = jnp.concatenate(
        [values[:, q * part : (q + 1) * part] for q in range(shares)], axis=0
    )
    select, values = select.T.astype(bf16), values.astype(bf16)
    step = held.shape[0] // sems.shape[0]
    copies = []
    for n in range(sems.shape[0]):
        place = pl.ds(n * step, step)
        held[place, :] = jnp.dot(
            select[n * step : (n + 1) * step], values, preferred_element_type=f32
        ).astype(bf16)
        copies.append(pltpu.make_async_copy(held.at[place], out_ref.at[place], sems.at[n]))
        copies[-1].start()
    for copy in copies:
        copy.wait()


def pack_rows(routes, rows, shares, experts):
    part = rows.shape[1] // shares
    total = experts * shares * CAP
    return pl.pallas_call(
        functools.partial(pack_kernel, shares, experts),
        out_shape=jax.ShapeDtypeStruct((total, part), rows.dtype),
        in_specs=[whole] * 2,
        out_specs=pl.BlockSpec(memory_space=pl.ANY),
        scratch_shapes=[
            pltpu.VMEM((total, part), rows.dtype),
            pltpu.SemaphoreType.DMA((4,)),
        ],
        compiler_params=pltpu.CompilerParams(vmem_limit_bytes=58 * 1024 * 1024),
        cost_estimate=pl.CostEstimate(
            flops=2 * total * part * rows.shape[0] * shares,
            bytes_accessed=2 * total * part,
            transcendentals=0,
        ),
    )(routes, rows)


def hidden_kernel(count, shares, *refs):
    halves, (order_ref, gate_ref, up_ref), ahead = refs[:count], refs[count : count + 3], refs[count + 3 : -2]
    out_ref, wide = refs[-2:]
    first = 0
    for ref in ahead:
        first = ref.shape[0]
        out_ref[pl.ds(0, first), :] = ref[...]
    rows, part = halves[0].shape
    slots = rows // shares
    for h in range(count):
        ordered = jnp.dot(
            order_ref[...], halves[h][...], preferred_element_type=jnp.float32
        ).astype(wide.dtype)
        for q in range(shares):
            wide[pl.ds(h * slots, slots), pl.ds(q * part, part)] = ordered[
                q * slots : (q + 1) * slots
            ]
    gate = jnp.dot(wide[...], gate_ref[...], preferred_element_type=jnp.float32)
    upper = jnp.dot(wide[...], up_ref[...], preferred_element_type=jnp.float32)
    out_ref[pl.ds(first, wide.shape[0]), :] = (gate / (1.0 + jnp.exp(-gate)) * upper).astype(
        out_ref.dtype
    )


def hidden_units(halves, order, w_gate, w_up, ahead):
    count = len(halves)
    rows, part = halves[0].shape
    width, units = w_gate.shape
    shares = width // part
    total = count * rows // shares
    return pl.pallas_call(
        functools.partial(hidden_kernel, count, shares),
        out_shape=jax.ShapeDtypeStruct(
            (total + sum(v.shape[0] for v in ahead), units), jnp.bfloat16
        ),
        in_specs=[whole] * (count + 3 + len(ahead)),
        out_specs=whole,
        scratch_shapes=[pltpu.VMEM((total, width), jnp.bfloat16)],
        compiler_params=vmem_params,
        cost_estimate=pl.CostEstimate(
            flops=4 * total * width * units,
            bytes_accessed=4 * width * units + 2 * total * width,
            transcendentals=total * units,
        ),
    )(*halves, order, w_gate, w_up, *ahead)


def stack_kernel(shares, *refs):
    weights, out_ref = refs[:shares], refs[shares]
    units = out_ref.shape[0] // shares
    for s in range(shares):
        out_ref[pl.ds(s * units, units), :] = weights[s][pl.ds(0, units), :]


def stack_shares(weights, units):
    shares, part = len(weights), weights[0].shape[1]
    return pl.pallas_call(
        functools.partial(stack_kernel, shares),
        out_shape=jax.ShapeDtypeStruct((shares * units, part), jnp.bfloat16),
        in_specs=[whole] * shares,
        out_specs=whole,
        compiler_params=vmem_params,
        cost_estimate=pl.CostEstimate(
            flops=0, bytes_accessed=4 * shares * units * part, transcendentals=0
        ),
    )(*weights)


def down_early_kernel(shares, *refs):
    early, weights_ref, out_ref = refs[:shares], refs[shares], refs[shares + 1]
    slots = out_ref.shape[0] // shares
    count = early[0].shape[1]
    for block in range(shares):
        total = None
        for s in range(shares):
            of_sender = (block - s) % shares
            if of_sender == shares // 2:
                continue
            place = of_sender - (of_sender > shares // 2)
            units = early[s][pl.ds(place * slots, slots), :]
            weights = weights_ref[pl.ds(s * count, count), :]
            term = jnp.dot(units, weights, preferred_element_type=jnp.float32)
            total = term if total is None else total + term
        out_ref[pl.ds(block * slots, slots), :] = total


def down_late_kernel(shares, *refs):
    late, (weights_ref, early_ref, order_ref, out_ref, plain, held, sems) = (
        refs[:shares],
        refs[shares:],
    )
    slots, count = late[0].shape
    half = slots // 2
    for block in range(shares):
        s = (block - shares // 2) % shares
        weights = weights_ref[pl.ds(s * count, count), :]
        term = jnp.dot(late[s][...], weights, preferred_element_type=jnp.float32)
        total = (early_ref[pl.ds(block * slots, slots), :] + term).astype(plain.dtype)
        plain[pl.ds(block * half, half), :] = total[:half]
        plain[pl.ds((shares + block) * half, half), :] = total[half:]
    copies = []
    for h in range(2):
        place = pl.ds(h * shares * half, shares * half)
        held[place, :] = jnp.dot(
            order_ref[...], plain[place, :], preferred_element_type=jnp.float32
        ).astype(held.dtype)
        copies.append(pltpu.make_async_copy(held.at[place], out_ref.at[place], sems.at[h]))
        copies[-1].start()
    for copy in copies:
        copy.wait()


def down_early(early, weights):
    shares = len(early)
    units, part = early[0].shape[1], weights.shape[1]
    rows = early[0].shape[0] // (shares - 1) * shares
    return pl.pallas_call(
        functools.partial(down_early_kernel, shares),
        out_shape=jax.ShapeDtypeStruct((rows, part), jnp.float32),
        in_specs=[whole] * (shares + 1),
        out_specs=whole,
        compiler_params=vmem_params,
        cost_estimate=pl.CostEstimate(
            flops=2 * rows * part * (shares - 1) * units,
            bytes_accessed=4 * rows * part + 2 * units * part * shares,
            transcendentals=0,
        ),
    )(*early, weights)


def down_late(late, weights, early, order):
    shares = len(late)
    rows, part = early.shape
    return pl.pallas_call(
        functools.partial(down_late_kernel, shares),
        out_shape=jax.ShapeDtypeStruct((rows, part), jnp.bfloat16),
        in_specs=[whole] * (shares + 3),
        out_specs=pl.BlockSpec(memory_space=pl.ANY),
        scratch_shapes=[
            pltpu.VMEM((rows, part), jnp.bfloat16),
            pltpu.VMEM((rows, part), jnp.bfloat16),
            pltpu.SemaphoreType.DMA((2,)),
        ],
        compiler_params=vmem_params,
        cost_estimate=pl.CostEstimate(
            flops=2 * rows * part * (late[0].shape[1] + rows),
            bytes_accessed=6 * rows * part,
            transcendentals=0,
        ),
    )(*late, weights, early, order)


def place_kernel(shares, first_ref, *refs):
    pieces, out_ref = refs[:shares], refs[shares]
    part = pieces[0].shape[1]
    for d in range(shares):
        quarter = lax.rem(first_ref[0] + d, shares)
        place = pl.ds(pl.multiple_of(quarter * part, 128), part)
        out_ref[:, place] = pieces[d][...]


def place_quarters(first, pieces):
    shares = len(pieces)
    rows, part = pieces[0].shape
    return pl.pallas_call(
        functools.partial(place_kernel, shares),
        out_shape=jax.ShapeDtypeStruct((rows, shares * part), pieces[0].dtype),
        in_specs=[pl.BlockSpec(memory_space=pltpu.SMEM)] + [whole] * shares,
        out_specs=whole,
        compiler_params=vmem_params,
        cost_estimate=pl.CostEstimate(
            flops=0, bytes_accessed=4 * rows * shares * part, transcendentals=0
        ),
    )(first.reshape(1), *pieces)


def gates_kernel(shares, chosen, *refs):
    f32 = jnp.float32
    infos, out_ref = refs[:shares], refs[shares]
    rows = out_ref.shape[0] // (3 * shares)
    lane = lax.broadcasted_iota(jnp.int32, (rows, out_ref.shape[1]), 1)
    chunk = shares * CAP
    expert, slot, block = lane // chunk, lane % CAP, lane % chunk // CAP
    expert, slot = expert.astype(f32), slot.astype(f32)
    before = lax.broadcasted_iota(jnp.int32, (rows, rows), 0) > lax.broadcasted_iota(
        jnp.int32, (rows, rows), 1
    )
    parts = []
    for d in range(shares):
        info = infos[d][...].astype(f32)[:rows]
        named = jnp.zeros(lane.shape, f32)
        gate = jnp.zeros(lane.shape, f32)
        for k in range(chosen):
            here = info[:, k : k + 1] == expert
            value = (info[:, chosen + k : chosen + k + 1] + info[:, 2 * chosen + k : 2 * chosen + k + 1]) + info[
                :, 3 * chosen + k : 3 * chosen + k + 1
            ]
            named = jnp.where(here, 1.0, named)
            gate = jnp.where(here, value, gate)
        earlier = jnp.dot(before.astype(f32), named, preferred_element_type=f32)
        taken = (earlier == slot) & (block == d)
        parts.append(jnp.where(taken, gate, 0.0))
    out_ref[...] = jnp.concatenate(split3(jnp.concatenate(parts, axis=0)), axis=0)


def gates_of_slots(infos, units, rows, chosen, experts):
    shares = len(infos)
    slots = experts * shares * CAP
    below = pl.BlockSpec((INFO, 128), lambda n: (units // INFO, 0))
    return pl.pallas_call(
        functools.partial(gates_kernel, shares, chosen),
        grid=(1,),
        out_shape=jax.ShapeDtypeStruct((3 * shares * rows, slots), jnp.bfloat16),
        in_specs=[below] * shares,
        out_specs=pl.BlockSpec((3 * shares * rows, slots), lambda n: (0, 0)),
        compiler_params=vmem_params,
        cost_estimate=pl.CostEstimate(flops=0, bytes_accessed=6 * shares * rows * slots, transcendentals=0),
    )(*infos)


def combine_kernel(shares, gates_ref, values_ref, *outs):
    sums = jnp.dot(gates_ref[...], values_ref[...], preferred_element_type=jnp.float32)
    count = sums.shape[0] // 3
    sums = sums[2 * count :] + sums[count : 2 * count] + sums[:count]
    rows = count // shares
    for d in range(shares):
        outs[d][...] = sums[d * rows : (d + 1) * rows].astype(outs[d].dtype)


def combine_slots(gates, values, shares):
    rows, part = gates.shape[0] // (3 * shares), values.shape[1]
    return pl.pallas_call(
        functools.partial(combine_kernel, shares),
        out_shape=(jax.ShapeDtypeStruct((rows, part), jnp.bfloat16),) * shares,
        in_specs=[whole] * 2,
        out_specs=(whole,) * shares,
        compiler_params=vmem_params,
        cost_estimate=pl.CostEstimate(
            flops=2 * gates.size * part, bytes_accessed=2 * values.size, transcendentals=0
        ),
    )(gates, values)


def per_device(
    query_latent,
    query_rope,
    cache_latent,
    cache_rope,
    cache_len,
    moe_input,
    routes,
    gate_weights,
    w_gate,
    w_up,
    w_down,
):
    bf16, f32 = jnp.bfloat16, jnp.float32
    shares = lax.axis_size("tensor")
    experts = lax.axis_size("expert")
    me = lax.axis_index("tensor")
    rows, width = moe_input.shape
    chosen = routes.shape[1]
    units = w_gate.shape[2]
    part = width // shares
    slots = experts * CAP

    def shift(value, by):
        pairs = [(i, (i + by) % shares) for i in range(shares)]
        return lax.ppermute(value, "tensor", pairs)

    packed = pack_rows(routes, moe_input, shares, experts)
    packed, w_down, routes, gate_weights = lax.optimization_barrier(
        (packed, w_down, routes, gate_weights)
    )
    received = lax.all_to_all(
        packed.reshape(experts, shares * CAP, part),
        "expert",
        split_axis=0,
        concat_axis=0,
        tiled=True,
    ).reshape(shares * slots, part)
    info = jnp.concatenate((routes.astype(bf16),) + split3(gate_weights), axis=1)
    info = jnp.pad(info, ((0, INFO - rows), (0, part - info.shape[1])))
    down_parts = [
        jnp.concatenate(
            [
                lax.dynamic_slice(w_down[0], (0, ((me + by) % shares) * part), (units, part)),
                info,
            ],
            axis=0,
        )
        for by in range(shares)
    ]
    down = [down_parts[0]] + [shift(down_parts[by], by) for by in range(1, shares)]
    local_context = attend(query_latent, query_rope, cache_latent, cache_rope, cache_len)
    heads, latent = local_context.shape[1:]
    received, local_context = lax.optimization_barrier((received, local_context))

    half = shares * slots // 2
    low, high = received[:half], received[half:]
    place = jnp.arange(half, dtype=jnp.int32)
    by_quarter = place // (half // shares), place % (half // shares)
    source = by_quarter[1] // CAP * (shares * CAP) + by_quarter[0] * CAP + by_quarter[1] % CAP
    sort = (source[:, None] == place[None, :]).astype(bf16)

    def hidden_of(*halves, ahead=()):
        return hidden_units(halves, sort, w_gate[0], w_up[0], ahead)

    low1, high3 = shift(low, 1), shift(high, 3)
    hidden0 = hidden_of(low, high)
    low, high, hidden0, down = lax.optimization_barrier((low, high, hidden0, down))
    high1, low3 = shift(high, 1), shift(low, 3)
    low2, high2 = shift(low1, 1), shift(high3, 3)
    early = hidden_of(low1, high1, low3, high3, ahead=(hidden0,))
    early, down = lax.optimization_barrier((early, down))
    stacked = stack_shares(down, units)
    early = [early] + [shift(early, by) for by in range(1, shares)]
    late = hidden_of(low2, high2)
    late = [late] + [shift(late, by) for by in range(1, shares)]

    expert_out = down_late(late, stacked, down_early(early, stacked), sort.T)
    expert_out, local_context, down = lax.optimization_barrier(
        (expert_out, local_context, down)
    )

    returned = lax.all_to_all(
        expert_out.reshape(experts, shares * CAP, part),
        "expert",
        split_axis=0,
        concat_axis=0,
        tiled=True,
    ).reshape(experts * shares * CAP, part)
    context_parts = [
        lax.dynamic_slice(
            local_context, (((me + by) % shares) * rows, 0, 0), (rows, heads, latent)
        )
        for by in range(shares)
    ]
    context_parts = [context_parts[0]] + [
        shift(context_parts[by], by) for by in range(1, shares)
    ]

    context = jnp.zeros((rows, shares, heads, latent), bf16)
    for by in range(shares):
        context = lax.dynamic_update_slice(
            context, context_parts[by][:, None], (0, (me - by) % shares, 0, 0)
        )

    combine = gates_of_slots(down, units, rows, chosen, experts)
    returned, context, combine = lax.optimization_barrier((returned, context, combine))
    sums = combine_slots(combine, returned, shares)
    pieces = [sums[0]] + [shift(sums[d], shares - d) for d in range(1, shares)]
    moe_output = place_quarters(me, pieces)
    return (context.reshape(rows, shares * heads, latent), moe_output)


def solution(mesh):
    return jax.shard_map(
        per_device,
        mesh=mesh,
        in_specs=(
            P("expert", "tensor", None),
            P("expert", "tensor"),
            P("expert", None, None),
            P("expert", None, None),
            P("expert"),
            P(("expert", "tensor"), None),
            P(("expert", "tensor"), None),
            P(("expert", "tensor"), None),
            P("expert", None, "tensor"),
            P("expert", None, "tensor"),
            P("expert", "tensor", None),
        ),
        out_specs=(P(("expert", "tensor"), None, None), P(("expert", "tensor"), None)),
        check_vma=False,
    )
```
